256 devices in a mesh: af: 32 (over y, z), vert: 8 (over x, core).
Axes of the slice: x: 4, y: 4, z: 8, core: 2. Of those that a mesh axis runs over, the one named last changes fastest.
Arguments:
- recorded: float32 [256, 64, 192], P('af', 'vert'), may hold values from -170 to 170, as said below
- kernel: float32 [256, 2, 96, 512], P('af'), may hold values from -0.1875 to 0.1875
- cutoff: int32 [512], replicated, may hold values from 128 to 512, as said below
Outputs:
- solution: float32 [64, 512, 512], P('vert', 'af')
- direction: float32 [64, 512, 512], P('vert', 'af')
- left_basis_vector: float32 [256, 64, 192], P('af', 'vert')
The draws below stay inside these ranges and needn't reach their ends.
Inputs may be any that keep to these rules, and one draw needn't show every extreme that they name: `recorded`: real parts fill the first 96 entries of the last dimension, imaginary parts the rest. `cutoff`: some receiver keeps all 512 samples and some receiver keeps a quarter of 512.
All inputs are finite; a program needn't handle non-finite values.
Results may differ from the reference program's by a relative error of at most 0.0045.
Values sent between devices are 32-bit elements; how exact they have to be, the bound alone decides.
No kernel may reach another device: no remote copies, remote signals or barrier semaphores. Data moves between devices by JAX's collectives and lax.ppermute only.
A program may use at most 64 MiB of HBM per device.

```python
import math
import jax
import jax.numpy as jnp
from jax import lax

VIRT = 64
SRCS = 96
FREQS = 256
SAMPLES = 512
RECV = 512
ITERS = 2


def draw_recorded(key, part):
    key = jax.random.fold_in(key, 11)
    key_noise, key_virt, key_src = jax.random.split(key, 3)
    shape_full = (FREQS, VIRT, 2 * SRCS)
    growth = jnp.exp(math.log(3.0) * jnp.arange(FREQS, dtype=jnp.float32) / (FREQS - 1))[:, None, None]
    virt_scale = jnp.exp(jax.random.uniform(key_virt, (1, VIRT, 1), jnp.float32, math.log(0.3), math.log(3.0)))
    src_scale = jnp.exp(jax.random.uniform(key_src, (1, 1, 2 * SRCS), jnp.float32, math.log(0.3), math.log(3.0)))
    noise = jnp.clip(jax.random.normal(key_noise, shape_full, jnp.float32), -6.0, 6.0)
    return (noise * growth * virt_scale * src_scale).astype(jnp.float32)


def draw_cutoff(key, part):
    key = jax.random.fold_in(key, 23)
    key_values, key_places = jax.random.split(key)
    values = jax.random.randint(key_values, (RECV,), SAMPLES // 4, SAMPLES + 1, dtype=jnp.int32)
    places = jax.random.permutation(key_places, RECV)
    receivers = jnp.arange(RECV, dtype=jnp.int32)
    values = jnp.where(receivers == places[0], SAMPLES, values)
    values = jnp.where(receivers == places[1], SAMPLES // 4, values)
    return values.astype(jnp.int32)


def block_levels(rng, dims, cuts, smallest, high):
    level = 1.0
    for axis_at, parts in cuts:
        steps = jax.random.uniform(jax.random.fold_in(jax.random.fold_in(rng, 6), axis_at), (parts,), jnp.float32, smallest / len(cuts), high / len(cuts))
        level = level * jnp.repeat(jnp.exp(steps), dims[axis_at] // parts).reshape((-1,) + (1,) * (len(dims) - 1 - axis_at))
    return level


def normal_values(own_key, shape, scale, reach, cuts=(), held_as=jnp.bfloat16):
    level = block_levels(own_key, shape, cuts, -0.22, 0.18) if cuts else 1.0
    result = jax.random.normal(own_key, shape, jnp.float32) * scale * level
    return jnp.minimum(jnp.maximum(result, -reach), reach).astype(held_as)


def setup_inputs(seed: int = 0) -> dict:
    key_list = jax.random.split(jax.random.key(seed), 4)
    return {
        "recorded": draw_recorded(jax.random.fold_in(key_list[3], 71), 0),
        "kernel": normal_values(key_list[1], (FREQS, 2, SRCS, RECV), (2 * RECV) ** -0.5, 0.1875, ((0, 32),), jnp.float32),
        "cutoff": draw_cutoff(jax.random.fold_in(key_list[3], 71), 0),
    }


EPSILON = 1e-06

def dft_table():
    times = jnp.arange(SAMPLES, dtype=jnp.int32)
    freq_index = jnp.arange(FREQS, dtype=jnp.int32)
    phases = times[:, None] * freq_index[None, :] % SAMPLES
    angles = 2.0 * math.pi / SAMPLES * phases.astype(jnp.float32)
    scale_factor = 1.0 / math.sqrt(SAMPLES)
    return jnp.concatenate([jnp.cos(angles), -jnp.sin(angles)], axis=1) * scale_factor

def contract_forward(operand_array, weight_factors):
    return jnp.einsum('pun,uln->upl', operand_array, weight_factors, precision=lax.Precision.HIGHEST)

def adjoint_contraction(operand_array, weight_factors):
    return jnp.einsum('xug,xge->uxe', operand_array, weight_factors, precision=lax.Precision.HIGHEST)

def kernel_apply(spectra, kernel):
    real_part = spectra[:, 0]
    imag_part = spectra[:, 1]
    kernel_real = kernel[:, 0]
    kernel_imag = kernel[:, 1]
    out_real = contract_forward(real_part, kernel_real) - contract_forward(imag_part, kernel_imag)
    out_imag = contract_forward(real_part, kernel_imag) + contract_forward(imag_part, kernel_real)
    return jnp.concatenate([out_real, out_imag], axis=2)

def kernel_adjoint(values, kernel):
    count = kernel.shape[2]
    real_part = values[:, :, :count]
    imag_part = values[:, :, count:]
    kernel_real = kernel[:, 0]
    kernel_imag = kernel[:, 1]
    out_real = adjoint_contraction(real_part, kernel_real) + adjoint_contraction(imag_part, kernel_imag)
    out_imag = adjoint_contraction(imag_part, kernel_real) - adjoint_contraction(real_part, kernel_imag)
    return jnp.stack([out_real, out_imag], axis=1)

def transform(pieces, fourier):
    return jnp.einsum('vtr,tk->vkr', pieces, fourier, precision=lax.Precision.HIGHEST)

def inverse(pieces, fourier):
    return jnp.einsum('vkr,tk->vtr', pieces, fourier, precision=lax.Precision.HIGHEST)

def global_norm(vector):
    return jnp.sqrt(jnp.sum(vector * vector) + EPSILON)

def reference(recorded, kernel, cutoff):
    fourier = dft_table()
    mask_model = (jnp.arange(SAMPLES, dtype=jnp.int32)[:, None] < cutoff[None, :]).astype(jnp.float32)

    def forward(vector):
        spectra = transform(vector * mask_model, fourier)
        return kernel_apply(spectra.reshape(VIRT, 2, FREQS, RECV), kernel)

    def adjoint(values):
        spread = kernel_adjoint(values, kernel)
        return inverse(spread.reshape(VIRT, 2 * FREQS, RECV), fourier) * mask_model
    beta_norm = global_norm(recorded)
    left_vec = recorded / beta_norm
    right_vec = adjoint(left_vec)
    alpha_norm = global_norm(right_vec)
    right_vec = right_vec / alpha_norm
    direction = right_vec
    solution = jnp.zeros_like(right_vec)
    phibar = beta_norm
    rhobar = alpha_norm
    for iteration in range(ITERS):
        left_vec = forward(right_vec) - alpha_norm * left_vec
        beta_norm = global_norm(left_vec)
        left_vec = left_vec / beta_norm
        right_vec = adjoint(left_vec) - beta_norm * right_vec
        alpha_norm = global_norm(right_vec)
        right_vec = right_vec / alpha_norm
        rho_value = jnp.sqrt(rhobar * rhobar + beta_norm * beta_norm)
        cosine = rhobar / rho_value
        sine_value = beta_norm / rho_value
        theta_value = sine_value * alpha_norm
        rhobar = -cosine * alpha_norm
        phi_value = cosine * phibar
        phibar = sine_value * phibar
        solution = solution + phi_value / rho_value * direction
        direction = right_vec - theta_value / rho_value * direction
    return (solution, direction, left_vec)
```

```python
import math

import jax
import jax.numpy as jnp
import numpy as np
from jax import lax
from jax.experimental import pallas as pl
from jax.experimental.pallas import tpu as pltpu
from jax.sharding import PartitionSpec as P

FREQS = 256
SAMPLES = 512
RECV = 512
SRCS = 96
EPSILON = 1e-06
F32 = jnp.float32
BF16 = jnp.bfloat16

AF = 32
VERT = 8
FB = FREQS // AF
VB = 8
QB = RECV // 128
KB = 2 * FB
MSG = KB + 1
TB = SAMPLES // AF
LAST = 3 * TB + 1
VMEM = 48 * 1024 * 1024


def dft_tables():
    times = np.arange(SAMPLES)
    freqs = np.arange(FREQS)
    angles = 2.0 * math.pi / SAMPLES * ((times[:, None] * freqs[None, :]) % SAMPLES)
    scale = 1.0 / math.sqrt(SAMPLES)
    table = np.stack([np.cos(angles), -np.sin(angles)], axis=2) * scale
    table = table.reshape(SAMPLES, 2 * FREQS).astype(np.float32)
    out = []
    for t in (table, np.ascontiguousarray(table.T)):
        hi = t.astype(jnp.bfloat16)
        out += [hi, (t - hi.astype(np.float32)).astype(jnp.bfloat16)]
    return out


def split(x):
    hi = x.astype(BF16)
    return hi, (x - hi.astype(F32)).astype(BF16)


def dot(a, b):
    return lax.dot_general(a, b, (((1,), (0,)), ((), ())), preferred_element_type=F32)


def dot_nt(a, b):
    return lax.dot_general(a, b, (((1,), (1,)), ((), ())), preferred_element_type=F32)


def turned(x, sign):
    return jnp.concatenate([sign * x[:, SRCS:], -sign * x[:, :SRCS]], axis=1)


def kernel_adjoint(u, khi, klo):
    hi, lo = split(jnp.concatenate([u, turned(u, 1.0)], axis=0))
    both = dot(jnp.concatenate([hi, lo], axis=0), khi)
    return both[: 2 * VB] + both[2 * VB :] + dot(hi, klo)


def kernel_forward(x, khi, klo):
    hi, lo = split(x)
    both = dot_nt(jnp.concatenate([hi, lo], axis=0), khi)
    y = both[: 2 * VB] + both[2 * VB :] + dot_nt(hi, klo)
    return y[:VB] + turned(y[VB:], -1.0)


def ratio(a, b):
    return jnp.where(b > 0, a / jnp.where(b > 0, b, 1.0), 0.0)


def arrived_sum(recv, pitch):
    rows = recv[pl.ds(pitch - 1, AF, stride=pitch), :]
    return jnp.broadcast_to(jnp.sum(rows, keepdims=True), (1, 128))


def lane_zero(total):
    lane = lax.broadcasted_iota(jnp.int32, (1, 128), 1)
    return jnp.where(lane == 0, jnp.broadcast_to(total, (1, 128)), 0.0)


def put_spectra(msg, f, z):
    for c in range(2):
        for q in range(QB):
            msg[pl.ds(q * MSG + 2 * f + c, VB, stride=QB * MSG), :] = z[
                c * VB : (c + 1) * VB, q * 128 : (q + 1) * 128
            ]


def put_partial(msg, row, pitch):
    for d in range(AF):
        msg[pl.ds(d * pitch + pitch - 1, 1), :] = row


def first_kernel(u_ref, k_ref, msg, khi_ref, klo_ref):
    square = jnp.zeros((VB, 2 * SRCS), F32)
    for f in range(FB):
        u = u_ref[f]
        square += u * u
        khi, klo = split(k_ref[f])
        khi_ref[f] = khi
        klo_ref[f] = klo
        put_spectra(msg, f, kernel_adjoint(u, khi, klo))
    put_partial(msg, lane_zero(jnp.sum(square, keepdims=True)), MSG)


def data_kernel(order, recv, khi_ref, klo_ref, before_ref, stats, msg, q_ref, stats_out):
    total = arrived_sum(recv, MSG)
    stats_out[...] = stats[...]
    stats_out[pl.ds(order, 1), :] = total
    coefficient = ratio(total, stats[pl.ds(order - 1, 1), :])[:, :1]
    square = jnp.zeros((VB, 2 * SRCS), F32)
    for f in range(FB):
        khi, klo = khi_ref[f], klo_ref[f]
        x = jnp.concatenate(
            [
                jnp.concatenate(
                    [
                        recv[pl.ds(q * MSG + 2 * f + c, VB, stride=QB * MSG), :]
                        for q in range(QB)
                    ],
                    axis=1,
                )
                for c in range(2)
            ],
            axis=0,
        )
        u = kernel_forward(x, khi, klo) - coefficient * before_ref[f]
        q_ref[f] = u
        square += u * u
        put_spectra(msg, f, kernel_adjoint(u, khi, klo))
    put_partial(msg, lane_zero(jnp.sum(square, keepdims=True)), MSG)


def table_apply(hi_ref, lo_ref, x):
    hi, lo = split(x)
    both = dot(hi_ref[...], jnp.concatenate([hi, lo], axis=1))
    return both[:, :128] + both[:, 128:] + dot(lo_ref[...], hi)


def model_kernel(order, last, *refs):
    refs = list(refs)
    recv, cut_ref, inv_hi, inv_lo = refs[:4]
    refs = refs[4:]
    if not last:
        fwd_hi, fwd_lo = refs[:2]
        refs = refs[2:]
    if order > 0:
        stats = refs.pop(0)
        earlier = [refs.pop(0) for _ in range(order // 2)]
    total = arrived_sum(recv, MSG)
    spectra = jnp.concatenate([recv[pl.ds(p * MSG, KB), :] for p in range(AF)], axis=0)
    s = table_apply(inv_hi, inv_lo, spectra)
    if order > 0:
        s = s - ratio(total, stats[pl.ds(order - 1, 1), :]) * earlier[-1][...]
    keep = lax.broadcasted_iota(jnp.int32, (SAMPLES, 128), 0) < cut_ref[...]
    s = jnp.where(keep, s, 0.0)
    partial = jnp.sum(s * s, axis=0, keepdims=True)
    if last:
        msg, stats_out = refs
    else:
        msg, s_ref, stats_out = refs
        s_ref[...] = s
    stats_out[...] = stats[...] if order > 0 else jnp.zeros((8, 128), F32)
    stats_out[pl.ds(order, 1), :] = total
    if last:
        for j, value in enumerate([e[...] for e in earlier] + [s]):
            for p in range(AF):
                msg[pl.ds(p * LAST + j * TB, TB), :] = value[p * TB : (p + 1) * TB]
        put_partial(msg, partial, LAST)
    else:
        out = table_apply(fwd_hi, fwd_lo, s)
        for p in range(AF):
            msg[pl.ds(p * MSG, KB), :] = out[p * KB : (p + 1) * KB]
        put_partial(msg, partial, MSG)


def stats_kernel(recv, stats, out):
    total = arrived_sum(recv, LAST)
    row = lax.broadcasted_iota(jnp.int32, (8, 128), 0)
    mine = jnp.where(row == 5, total, stats[...])
    for g in range(VERT):
        out[pl.ds(8 * g, 8), :] = mine


def last_kernel(group_ref, recv, gathered, q0_ref, q1_ref, q2_ref, sol_ref, dir_ref, left_ref, rows):
    n0, m1, n1, m2, n2, m3 = [gathered[pl.ds(j, VERT, stride=8), :] for j in range(6)]

    def norm(x):
        return jnp.sqrt(jnp.sum(x, axis=0, keepdims=True) + EPSILON)

    theta, kappa, lam, mu = ratio(m1, n0), ratio(n1, m1), ratio(m2, n1), ratio(n2, m2)
    beta0 = norm(n0)
    alpha1 = norm(m1 / (beta0 * beta0))
    e = 1.0 / (beta0 * alpha1)
    d = e * theta - alpha1 / beta0
    beta1 = norm(e * e * n1 + d * d * n0)
    f1 = e / beta1
    f0 = d / beta1
    h = f1 * kappa + f0 - beta1 * e
    alpha2 = norm(f1 * f1 * m2 + h * h * m1)
    g2 = f1 / alpha2
    g1 = h / alpha2
    rho1 = jnp.sqrt(alpha1 * alpha1 + beta1 * beta1)
    cos1, sin1 = alpha1 / rho1, beta1 / rho1
    theta1 = sin1 * alpha2
    rhobar = -cos1 * alpha2
    phi1, phibar = cos1 * beta0, sin1 * beta0
    w2 = g2
    w1 = g1 - theta1 / rho1 * e
    c2 = g2
    c1 = g2 * lam + g1 - alpha2 * f1
    c0 = g1 * theta - alpha2 * f0
    beta2 = norm(c2 * c2 * n2 + c1 * c1 * n1 + c0 * c0 * n0)
    c2, c1, c0 = c2 / beta2, c1 / beta2, c0 / beta2
    z3 = c2
    z2 = c2 * mu + c1 - beta2 * g2
    z1 = c1 * kappa + c0 - beta2 * g1
    alpha3 = norm(z3 * z3 * m3 + z2 * z2 * m2 + z1 * z1 * m1)
    rho2 = jnp.sqrt(rhobar * rhobar + beta2 * beta2)
    cos2, sin2 = rhobar / rho2, beta2 / rho2
    step2 = cos2 * phibar / rho2
    turn2 = sin2 * alpha3 / rho2
    x1 = phi1 / rho1 * e + step2 * w1
    x2 = step2 * w2
    y1 = z1 / alpha3 - turn2 * w1
    y2 = z2 / alpha3 - turn2 * w2
    y3 = z3 / alpha3
    for j, value in enumerate((x1, x2, y1, y2, y3, c0, c1, c2)):
        rows[pl.ds(8 * j, 8), :] = jnp.broadcast_to(value, (VERT, 128))
    group = group_ref[0]
    x1, x2, y1, y2, y3, c0, c1, c2 = [rows[pl.ds(8 * j + group, 1), :] for j in range(8)]
    for v in range(VB):
        for q in range(QB):
            at = (v * QB + q) * LAST
            s1, s2, s3 = [recv[pl.ds(at + j * TB, TB), :] for j in range(3)]
            sol_ref[v, :, q * 128 : (q + 1) * 128] = x1 * s1 + x2 * s2
            dir_ref[v, :, q * 128 : (q + 1) * 128] = y1 * s1 + y2 * s2 + y3 * s3
    c0, c1, c2 = c0[:, :1], c1[:, :1], c2[:, :1]
    for f in range(FB):
        left_ref[f] = c0 * q0_ref[f] + c1 * q1_ref[f] + c2 * q2_ref[f]


def call(body, outs, *operands, scratch=(), smem=0):
    vmem = pl.BlockSpec(memory_space=pltpu.VMEM)
    return pl.pallas_call(
        body,
        out_shape=[jax.ShapeDtypeStruct(s, t) for s, t in outs],
        in_specs=[pl.BlockSpec(memory_space=pltpu.SMEM)] * smem + [vmem] * (len(operands) - smem),
        out_specs=[vmem] * len(outs),
        scratch_shapes=list(scratch),
        compiler_params=pltpu.CompilerParams(vmem_limit_bytes=VMEM),
    )(*operands)


def exchange(message):
    return lax.all_to_all(message, "af", split_axis=0, concat_axis=0, tiled=True)


def per_device(recorded, kernel, cutoff):
    import functools

    inv_hi, inv_lo, fwd_hi, fwd_lo = [jnp.asarray(t) for t in dft_tables()]
    place = lax.axis_index("af")
    cut = lax.dynamic_slice(cutoff.reshape(QB, 128), (place % QB, 0), (1, 128))
    kernel = kernel.reshape(FB, 2 * SRCS, RECV)
    message = ((AF * MSG, 128), F32)
    data = ((FB, VB, 2 * SRCS), F32)
    model = ((SAMPLES, 128), F32)
    stat = ((8, 128), F32)
    wide = ((FB, 2 * SRCS, RECV), BF16)

    msg, khi, klo = call(first_kernel, [message, wide, wide], recorded, kernel)
    msg, s1, stats = call(
        functools.partial(model_kernel, 0, False),
        [message, model, stat],
        exchange(msg), cut, inv_hi, inv_lo, fwd_hi, fwd_lo,
    )
    msg, q1, stats = call(
        functools.partial(data_kernel, 1),
        [message, data, stat],
        exchange(msg), khi, klo, recorded, stats,
    )
    msg, s2, stats = call(
        functools.partial(model_kernel, 2, False),
        [message, model, stat],
        exchange(msg), cut, inv_hi, inv_lo, fwd_hi, fwd_lo, stats, s1,
    )
    msg, q2, stats = call(
        functools.partial(data_kernel, 3),
        [message, data, stat],
        exchange(msg), khi, klo, q1, stats,
    )
    msg, stats = call(
        functools.partial(model_kernel, 4, True),
        [((AF * LAST, 128), F32), stat],
        exchange(msg), cut, inv_hi, inv_lo, stats, s1, s2,
    )
    arrived = exchange(msg)
    [stats] = call(stats_kernel, [((VERT * 8, 128), F32)], arrived, stats)
    gathered = lax.all_to_all(stats, "vert", split_axis=0, concat_axis=0, tiled=True)
    group = lax.axis_index("vert").astype(jnp.int32).reshape(1)
    out = ((VB, TB, RECV), F32)
    return tuple(
        call(
            last_kernel,
            [out, out, data],
            group, arrived, gathered, recorded, q1, q2,
            scratch=[pltpu.VMEM((64, 128), F32)],
            smem=1,
        )
    )


def solution(mesh):
    in_specs = (P("af", "vert", None), P("af", None, None, None), P())
    out_specs = (P("vert", "af", None), P("vert", "af", None), P("af", "vert", None))
    return jax.shard_map(
        per_device, mesh=mesh, in_specs=in_specs, out_specs=out_specs, check_vma=False
    )
```

```python
import math

import jax
import jax.numpy as jnp
import numpy as np
from jax import lax
from jax.experimental import pallas as pl
from jax.experimental.pallas import tpu as pltpu
from jax.sharding import PartitionSpec as P

FREQS = 256
SAMPLES = 512
RECV = 512
SRCS = 96
EPSILON = 1e-06
F32 = jnp.float32
BF16 = jnp.bfloat16

AF = 32
VERT = 8
FB = FREQS // AF
VB = 8
QB = RECV // 128
KB = 2 * FB
MSG = KB + 1
TB = SAMPLES // AF
LAST = 3 * TB + 1
VMEM = 16 * 1024 * 1024


def dft_tables():
    times = np.arange(SAMPLES)
    freqs = np.arange(FREQS)
    angles = 2.0 * math.pi / SAMPLES * ((times[:, None] * freqs[None, :]) % SAMPLES)
    scale = 1.0 / math.sqrt(SAMPLES)
    table = np.stack([np.cos(angles), -np.sin(angles)], axis=2) * scale
    table = table.reshape(SAMPLES, 2 * FREQS).astype(np.float32)
    out = []
    for t in (table, np.ascontiguousarray(table.T)):
        hi = t.astype(jnp.bfloat16)
        out += [hi, (t - hi.astype(np.float32)).astype(jnp.bfloat16)]
    return out


def split(x):
    hi = x.astype(BF16)
    return hi, (x - hi.astype(F32)).astype(BF16)


def dot(a, b):
    return lax.dot_general(a, b, (((1,), (0,)), ((), ())), preferred_element_type=F32)


def dot_nt(a, b):
    return lax.dot_general(a, b, (((1,), (1,)), ((), ())), preferred_element_type=F32)


def turned(x, sign):
    return jnp.concatenate([sign * x[:, SRCS:], -sign * x[:, :SRCS]], axis=1)


def kernel_adjoint(u, khi, klo):
    hi, lo = split(jnp.concatenate([u, turned(u, 1.0)], axis=0))
    both = dot(jnp.concatenate([hi, lo], axis=0), khi)
    return both[: 2 * VB] + both[2 * VB :] + dot(hi, klo)


def kernel_forward(x, khi, klo):
    hi, lo = split(x)
    both = dot_nt(jnp.concatenate([hi, lo], axis=0), khi)
    y = both[: 2 * VB] + both[2 * VB :] + dot_nt(hi, klo)
    return y[:VB] + turned(y[VB:], -1.0)


def ratio(a, b):
    return jnp.where(b > 0, a / jnp.where(b > 0, b, 1.0), 0.0)


def arrived_sum(recv, pitch):
    rows = recv[pl.ds(pitch - 1, AF, stride=pitch), :]
    return jnp.broadcast_to(jnp.sum(rows, keepdims=True), (1, 128))


def lane_zero(total):
    lane = lax.broadcasted_iota(jnp.int32, (1, 128), 1)
    return jnp.where(lane == 0, jnp.broadcast_to(total, (1, 128)), 0.0)


def put_spectra(msg, f, z):
    for c in range(2):
        for q in range(QB):
            msg[pl.ds(q * MSG + 2 * f + c, VB, stride=QB * MSG), :] = z[
                c * VB : (c + 1) * VB, q * 128 : (q + 1) * 128
            ]


def put_partial(msg, row, pitch):
    for d in range(AF):
        msg[pl.ds(d * pitch + pitch - 1, 1), :] = row


def first_kernel(u_ref, k_ref, msg, khi_ref, klo_ref):
    square = jnp.zeros((VB, 2 * SRCS), F32)
    for f in range(FB):
        u = u_ref[f]
        square += u * u
        khi, klo = split(k_ref[f])
        khi_ref[f] = khi
        klo_ref[f] = klo
        put_spectra(msg, f, kernel_adjoint(u, khi, klo))
    put_partial(msg, lane_zero(jnp.sum(square, keepdims=True)), MSG)


def data_kernel(order, recv, khi_ref, klo_ref, before_ref, stats, msg, q_ref, stats_out):
    total = arrived_sum(recv, MSG)
    stats_out[...] = stats[...]
    stats_out[pl.ds(order, 1), :] = total
    coefficient = ratio(total, stats[pl.ds(order - 1, 1), :])[:, :1]
    square = jnp.zeros((VB, 2 * SRCS), F32)
    for f in range(FB):
        khi, klo = khi_ref[f], klo_ref[f]
        x = jnp.concatenate(
            [
                jnp.concatenate(
                    [
                        recv[pl.ds(q * MSG + 2 * f + c, VB, stride=QB * MSG), :]
                        for q in range(QB)
                    ],
                    axis=1,
                )
                for c in range(2)
            ],
            axis=0,
        )
        u = kernel_forward(x, khi, klo) - coefficient * before_ref[f]
        q_ref[f] = u
        square += u * u
        put_spectra(msg, f, kernel_adjoint(u, khi, klo))
    put_partial(msg, lane_zero(jnp.sum(square, keepdims=True)), MSG)


def table_apply(hi_ref, lo_ref, x):
    hi, lo = split(x)
    both = dot(hi_ref[...], jnp.concatenate([hi, lo], axis=1))
    return both[:, :128] + both[:, 128:] + dot(lo_ref[...], hi)


def model_kernel(order, last, *refs):
    refs = list(refs)
    recv, cut_ref, inv_hi, inv_lo = refs[:4]
    refs = refs[4:]
    if not last:
        fwd_hi, fwd_lo = refs[:2]
        refs = refs[2:]
    if order > 0:
        stats = refs.pop(0)
        earlier = [refs.pop(0) for _ in range(order // 2)]
    total = arrived_sum(recv, MSG)
    spectra = jnp.concatenate([recv[pl.ds(p * MSG, KB), :] for p in range(AF)], axis=0)
    s = table_apply(inv_hi, inv_lo, spectra)
    if order > 0:
        s = s - ratio(total, stats[pl.ds(order - 1, 1), :]) * earlier[-1][...]
    keep = lax.broadcasted_iota(jnp.int32, (SAMPLES, 128), 0) < cut_ref[...]
    s = jnp.where(keep, s, 0.0)
    partial = jnp.sum(s * s, axis=0, keepdims=True)
    if last:
        msg, stats_out = refs
    else:
        msg, s_ref, stats_out = refs
        s_ref[...] = s
    stats_out[...] = stats[...] if order > 0 else jnp.zeros((8, 128), F32)
    stats_out[pl.ds(order, 1), :] = total
    if last:
        for j, value in enumerate([e[...] for e in earlier] + [s]):
            for p in range(AF):
                msg[pl.ds(p * LAST + j * TB, TB), :] = value[p * TB : (p + 1) * TB]
        put_partial(msg, partial, LAST)
    else:
        out = table_apply(fwd_hi, fwd_lo, s)
        for p in range(AF):
            msg[pl.ds(p * MSG, KB), :] = out[p * KB : (p + 1) * KB]
        put_partial(msg, partial, MSG)


def stats_kernel(recv, stats, out):
    total = arrived_sum(recv, LAST)
    row = lax.broadcasted_iota(jnp.int32, (8, 128), 0)
    mine = jnp.where(row == 5, total, stats[...])
    for g in range(VERT):
        out[pl.ds(8 * g, 8), :] = mine


def last_kernel(group_ref, recv, gathered, q0_ref, q1_ref, q2_ref, sol_ref, dir_ref, left_ref, rows):
    n0, m1, n1, m2, n2, m3 = [gathered[pl.ds(j, VERT, stride=8), :] for j in range(6)]

    def norm(x):
        return jnp.sqrt(jnp.sum(x, axis=0, keepdims=True) + EPSILON)

    theta, kappa, lam, mu = ratio(m1, n0), ratio(n1, m1), ratio(m2, n1), ratio(n2, m2)
    beta0 = norm(n0)
    alpha1 = norm(m1 / (beta0 * beta0))
    e = 1.0 / (beta0 * alpha1)
    d = e * theta - alpha1 / beta0
    beta1 = norm(e * e * n1 + d * d * n0)
    f1 = e / beta1
    f0 = d / beta1
    h = f1 * kappa + f0 - beta1 * e
    alpha2 = norm(f1 * f1 * m2 + h * h * m1)
    g2 = f1 / alpha2
    g1 = h / alpha2
    rho1 = jnp.sqrt(alpha1 * alpha1 + beta1 * beta1)
    cos1, sin1 = alpha1 / rho1, beta1 / rho1
    theta1 = sin1 * alpha2
    rhobar = -cos1 * alpha2
    phi1, phibar = cos1 * beta0, sin1 * beta0
    w2 = g2
    w1 = g1 - theta1 / rho1 * e
    c2 = g2
    c1 = g2 * lam + g1 - alpha2 * f1
    c0 = g1 * theta - alpha2 * f0
    beta2 = norm(c2 * c2 * n2 + c1 * c1 * n1 + c0 * c0 * n0)
    c2, c1, c0 = c2 / beta2, c1 / beta2, c0 / beta2
    z3 = c2
    z2 = c2 * mu + c1 - beta2 * g2
    z1 = c1 * kappa + c0 - beta2 * g1
    alpha3 = norm(z3 * z3 * m3 + z2 * z2 * m2 + z1 * z1 * m1)
    rho2 = jnp.sqrt(rhobar * rhobar + beta2 * beta2)
    cos2, sin2 = rhobar / rho2, beta2 / rho2
    step2 = cos2 * phibar / rho2
    turn2 = sin2 * alpha3 / rho2
    x1 = phi1 / rho1 * e + step2 * w1
    x2 = step2 * w2
    y1 = z1 / alpha3 - turn2 * w1
    y2 = z2 / alpha3 - turn2 * w2
    y3 = z3 / alpha3
    for j, value in enumerate((x1, x2, y1, y2, y3, c0, c1, c2)):
        rows[pl.ds(8 * j, 8), :] = jnp.broadcast_to(value, (VERT, 128))
    group = group_ref[0]
    x1, x2, y1, y2, y3, c0, c1, c2 = [rows[pl.ds(8 * j + group, 1), :] for j in range(8)]
    for v in range(VB):
        for q in range(QB):
            at = (v * QB + q) * LAST
            s1, s2, s3 = [recv[pl.ds(at + j * TB, TB), :] for j in range(3)]
            sol_ref[v, :, q * 128 : (q + 1) * 128] = x1 * s1 + x2 * s2
            dir_ref[v, :, q * 128 : (q + 1) * 128] = y1 * s1 + y2 * s2 + y3 * s3
    c0, c1, c2 = c0[:, :1], c1[:, :1], c2[:, :1]
    for f in range(FB):
        left_ref[f] = c0 * q0_ref[f] + c1 * q1_ref[f] + c2 * q2_ref[f]


def call(body, outs, *operands, scratch=(), smem=0):
    vmem = pl.BlockSpec(memory_space=pltpu.VMEM)
    return pl.pallas_call(
        body,
        out_shape=[jax.ShapeDtypeStruct(s, t) for s, t in outs],
        in_specs=[pl.BlockSpec(memory_space=pltpu.SMEM)] * smem + [vmem] * (len(operands) - smem),
        out_specs=[vmem] * len(outs),
        scratch_shapes=list(scratch),
        compiler_params=pltpu.CompilerParams(vmem_limit_bytes=VMEM),
    )(*operands)


def exchange(message):
    flat = message.reshape(AF, 1, message.shape[0] // AF * 128)
    return lax.all_to_all(flat, "af", split_axis=0, concat_axis=0, tiled=True).reshape(message.shape)


def per_device(recorded, kernel, cutoff):
    import functools

    inv_hi, inv_lo, fwd_hi, fwd_lo = [jnp.asarray(t) for t in dft_tables()]
    place = lax.axis_index("af")
    cut = lax.dynamic_slice(cutoff.reshape(QB, 128), (place % QB, 0), (1, 128))
    kernel = kernel.reshape(FB, 2 * SRCS, RECV)
    message = ((AF * MSG, 128), F32)
    data = ((FB, VB, 2 * SRCS), F32)
    model = ((SAMPLES, 128), F32)
    stat = ((8, 128), F32)
    wide = ((FB, 2 * SRCS, RECV), BF16)

    msg, khi, klo = call(first_kernel, [message, wide, wide], recorded, kernel)
    msg, s1, stats = call(
        functools.partial(model_kernel, 0, False),
        [message, model, stat],
        exchange(msg), cut, inv_hi, inv_lo, fwd_hi, fwd_lo,
    )
    msg, q1, stats = call(
        functools.partial(data_kernel, 1),
        [message, data, stat],
        exchange(msg), khi, klo, recorded, stats,
    )
    msg, s2, stats = call(
        functools.partial(model_kernel, 2, False),
        [message, model, stat],
        exchange(msg), cut, inv_hi, inv_lo, fwd_hi, fwd_lo, stats, s1,
    )
    msg, q2, stats = call(
        functools.partial(data_kernel, 3),
        [message, data, stat],
        exchange(msg), khi, klo, q1, stats,
    )
    msg, stats = call(
        functools.partial(model_kernel, 4, True),
        [((AF * LAST, 128), F32), stat],
        exchange(msg), cut, inv_hi, inv_lo, stats, s1, s2,
    )
    arrived = exchange(msg)
    [stats] = call(stats_kernel, [((VERT * 8, 128), F32)], arrived, stats)
    gathered = lax.all_to_all(stats, "vert", split_axis=0, concat_axis=0, tiled=True)
    group = lax.axis_index("vert").astype(jnp.int32).reshape(1)
    out = ((VB, TB, RECV), F32)
    return tuple(
        call(
            last_kernel,
            [out, out, data],
            group, arrived, gathered, recorded, q1, q2,
            scratch=[pltpu.VMEM((64, 128), F32)],
            smem=1,
        )
    )


def solution(mesh):
    in_specs = (P("af", "vert", None), P("af", None, None, None), P())
    out_specs = (P("vert", "af", None), P("vert", "af", None), P("af", "vert", None))
    return jax.shard_map(
        per_device, mesh=mesh, in_specs=in_specs, out_specs=out_specs, check_vma=False
    )
```

```python
import functools
import math

import jax
import jax.numpy as jnp
import numpy as np
from jax import lax
from jax.experimental import pallas as pl
from jax.experimental.pallas import tpu as pltpu
from jax.sharding import PartitionSpec as P

FREQS = 256
SAMPLES = 512
RECV = 512
SRCS = 96
EPSILON = 1e-06
F32 = jnp.float32
BF16 = jnp.bfloat16

AF = 32
VERT = 8
FB = FREQS // AF
VB = 8
QB = RECV // 128
KB = 2 * FB
MSG = KB + 1
TB = SAMPLES // AF
LAST = 3 * TB + 1


def dft_tables():
    times = np.arange(SAMPLES)
    freqs = np.arange(FREQS)
    angles = 2.0 * math.pi / SAMPLES * ((times[:, None] * freqs[None, :]) % SAMPLES)
    scale = 1.0 / math.sqrt(SAMPLES)
    table = np.stack([np.cos(angles), -np.sin(angles)], axis=2) * scale
    table = table.reshape(SAMPLES, 2 * FREQS).astype(np.float32)
    out = []
    for t in (table, np.ascontiguousarray(table.T)):
        hi = t.astype(jnp.bfloat16)
        out += [hi, (t - hi.astype(np.float32)).astype(jnp.bfloat16)]
    return np.stack(out)


def split(x):
    hi = x.astype(BF16)
    return hi, (x - hi.astype(F32)).astype(BF16)


def dot(a, b):
    return lax.dot_general(a, b, (((1,), (0,)), ((), ())), preferred_element_type=F32)


def dot_nt(a, b):
    return lax.dot_general(a, b, (((1,), (1,)), ((), ())), preferred_element_type=F32)


def turned(x, sign):
    return jnp.concatenate([sign * x[:, SRCS:], -sign * x[:, :SRCS]], axis=1)


def kernel_adjoint(u, khi, klo):
    hi, lo = split(jnp.concatenate([u, turned(u, 1.0)], axis=0))
    both = dot(jnp.concatenate([hi, lo], axis=0), khi)
    return both[: 2 * VB] + both[2 * VB :] + dot(hi, klo)


def kernel_forward(x, khi, klo):
    hi, lo = split(x)
    both = dot_nt(jnp.concatenate([hi, lo], axis=0), khi)
    y = both[: 2 * VB] + both[2 * VB :] + dot_nt(hi, klo)
    return y[:VB] + turned(y[VB:], -1.0)


def ratio(a, b):
    return jnp.where(b > 0, a / jnp.where(b > 0, b, 1.0), 0.0)


def arrived_sum(recv, pitch):
    rows = recv[pl.ds(pitch - 1, AF, stride=pitch), :]
    return jnp.broadcast_to(jnp.sum(rows, keepdims=True), (1, 128))


def lane_zero(total):
    lane = lax.broadcasted_iota(jnp.int32, (1, 128), 1)
    return jnp.where(lane == 0, jnp.broadcast_to(total, (1, 128)), 0.0)


def put_spectra(msg, f, z):
    for c in range(2):
        for q in range(QB):
            msg[pl.ds(q * MSG + 2 * f + c, VB, stride=QB * MSG), :] = z[
                c * VB : (c + 1) * VB, q * 128 : (q + 1) * 128
            ]


def put_partial(msg, row, pitch):
    for d in range(AF):
        msg[pl.ds(d * pitch + pitch - 1, 1), :] = row


def first_kernel(u_hbm, k_hbm, t_hbm, msg, khi_ref, klo_ref, t_ref, u_buf, k_buf, sems):
    u_copy = pltpu.make_async_copy(u_hbm, u_buf, sems.at[FB])
    k_copies = [pltpu.make_async_copy(k_hbm.at[f], k_buf.at[f], sems.at[f]) for f in range(FB)]
    t_copy = pltpu.make_async_copy(t_hbm, t_ref, sems.at[FB + 1])
    u_copy.start()
    for copy in k_copies:
        copy.start()
    t_copy.start()
    u_copy.wait()
    square = jnp.zeros((VB, 2 * SRCS), F32)
    for f in range(FB):
        u = u_buf[f]
        square += u * u
        k_copies[f].wait()
        khi, klo = split(k_buf[f])
        khi_ref[f] = khi
        klo_ref[f] = klo
        put_spectra(msg, f, kernel_adjoint(u, khi, klo))
    put_partial(msg, lane_zero(jnp.sum(square, keepdims=True)), MSG)
    t_copy.wait()


def data_kernel(order, recv, khi_ref, klo_ref, before_ref, stats, msg, q_ref, stats_out):
    total = arrived_sum(recv, MSG)
    stats_out[...] = stats[...]
    stats_out[pl.ds(order, 1), :] = total
    coefficient = ratio(total, stats[pl.ds(order - 1, 1), :])[:, :1]
    square = jnp.zeros((VB, 2 * SRCS), F32)
    steps = []
    for f in range(FB):
        x = jnp.concatenate(
            [
                jnp.concatenate(
                    [
                        recv[pl.ds(q * MSG + 2 * f + c, VB, stride=QB * MSG), :]
                        for q in range(QB)
                    ],
                    axis=1,
                )
                for c in range(2)
            ],
            axis=0,
        )
        u = kernel_forward(x, khi_ref[f], klo_ref[f]) - coefficient * before_ref[f]
        q_ref[f] = u
        square += u * u
        steps.append(u)
    for f in range(FB):
        put_spectra(msg, f, kernel_adjoint(steps[f], khi_ref[f], klo_ref[f]))
    put_partial(msg, lane_zero(jnp.sum(square, keepdims=True)), MSG)


def table_apply(table_ref, at, x):
    hi, lo = split(x)
    both = dot(table_ref[at], jnp.concatenate([hi, lo], axis=1))
    return both[:, :128] + both[:, 128:] + dot(table_ref[at + 1], hi)


def model_kernel(order, last, *refs):
    refs = list(refs)
    recv, cut_ref, table_ref = refs[:3]
    refs = refs[3:]
    if order > 0:
        stats = refs.pop(0)
        earlier = [refs.pop(0) for _ in range(order // 2)]
    total = arrived_sum(recv, MSG)
    spectra = jnp.concatenate([recv[pl.ds(p * MSG, KB), :] for p in range(AF)], axis=0)
    s = table_apply(table_ref, 0, spectra)
    if order > 0:
        s = s - ratio(total, stats[pl.ds(order - 1, 1), :]) * earlier[-1][...]
    cut = cut_ref[pl.ds(lax.rem(lax.axis_index("af"), QB), 1), :]
    keep = lax.broadcasted_iota(jnp.int32, (SAMPLES, 128), 0) < cut
    s = jnp.where(keep, s, 0.0)
    partial = jnp.sum(s * s, axis=0, keepdims=True)
    if last:
        msg, stats_out = refs
    else:
        msg, s_ref, stats_out = refs
        s_ref[...] = s
    stats_out[...] = stats[...] if order > 0 else jnp.zeros((8, 128), F32)
    stats_out[pl.ds(order, 1), :] = total
    if last:
        for j, value in enumerate([e[...] for e in earlier] + [s]):
            for p in range(AF):
                msg[pl.ds(p * LAST + j * TB, TB), :] = value[p * TB : (p + 1) * TB]
        put_partial(msg, partial, LAST)
    else:
        out = table_apply(table_ref, 2, s)
        for p in range(AF):
            msg[pl.ds(p * MSG, KB), :] = out[p * KB : (p + 1) * KB]
        put_partial(msg, partial, MSG)


def stats_kernel(recv, stats, out):
    total = arrived_sum(recv, LAST)
    row = lax.broadcasted_iota(jnp.int32, (8, 128), 0)
    mine = jnp.where(row == 5, total, stats[...])
    for g in range(VERT):
        out[pl.ds(8 * g, 8), :] = mine


def last_kernel(recv, gathered, q0_ref, q1_ref, q2_ref, sol_ref, dir_ref, left_ref, rows):
    n0, m1, n1, m2, n2, m3 = [gathered[pl.ds(j, VERT, stride=8), :] for j in range(6)]

    def norm(x):
        return jnp.sqrt(jnp.sum(x, axis=0, keepdims=True) + EPSILON)

    theta, kappa, lam, mu = ratio(m1, n0), ratio(n1, m1), ratio(m2, n1), ratio(n2, m2)
    beta0 = norm(n0)
    alpha1 = norm(m1 / (beta0 * beta0))
    e = 1.0 / (beta0 * alpha1)
    d = e * theta - alpha1 / beta0
    beta1 = norm(e * e * n1 + d * d * n0)
    f1 = e / beta1
    f0 = d / beta1
    h = f1 * kappa + f0 - beta1 * e
    alpha2 = norm(f1 * f1 * m2 + h * h * m1)
    g2 = f1 / alpha2
    g1 = h / alpha2
    rho1 = jnp.sqrt(alpha1 * alpha1 + beta1 * beta1)
    cos1, sin1 = alpha1 / rho1, beta1 / rho1
    theta1 = sin1 * alpha2
    rhobar = -cos1 * alpha2
    phi1, phibar = cos1 * beta0, sin1 * beta0
    w2 = g2
    w1 = g1 - theta1 / rho1 * e
    c2 = g2
    c1 = g2 * lam + g1 - alpha2 * f1
    c0 = g1 * theta - alpha2 * f0
    beta2 = norm(c2 * c2 * n2 + c1 * c1 * n1 + c0 * c0 * n0)
    c2, c1, c0 = c2 / beta2, c1 / beta2, c0 / beta2
    z3 = c2
    z2 = c2 * mu + c1 - beta2 * g2
    z1 = c1 * kappa + c0 - beta2 * g1
    alpha3 = norm(z3 * z3 * m3 + z2 * z2 * m2 + z1 * z1 * m1)
    rho2 = jnp.sqrt(rhobar * rhobar + beta2 * beta2)
    cos2, sin2 = rhobar / rho2, beta2 / rho2
    step2 = cos2 * phibar / rho2
    turn2 = sin2 * alpha3 / rho2
    x1 = phi1 / rho1 * e + step2 * w1
    x2 = step2 * w2
    y1 = z1 / alpha3 - turn2 * w1
    y2 = z2 / alpha3 - turn2 * w2
    y3 = z3 / alpha3
    for j, value in enumerate((x1, x2, y1, y2, y3, c0, c1, c2)):
        rows[pl.ds(8 * j, 8), :] = jnp.broadcast_to(value, (VERT, 128))
    group = lax.axis_index("vert")
    x1, x2, y1, y2, y3, c0, c1, c2 = [rows[pl.ds(8 * j + group, 1), :] for j in range(8)]
    for v in range(VB):
        for q in range(QB):
            at = (v * QB + q) * LAST
            s1, s2, s3 = [recv[pl.ds(at + j * TB, TB), :] for j in range(3)]
            sol_ref[v, :, q * 128 : (q + 1) * 128] = x1 * s1 + x2 * s2
            dir_ref[v, :, q * 128 : (q + 1) * 128] = y1 * s1 + y2 * s2 + y3 * s3
    c0, c1, c2 = c0[:, :1], c1[:, :1], c2[:, :1]
    for f in range(FB):
        left_ref[f] = c0 * q0_ref[f] + c1 * q1_ref[f] + c2 * q2_ref[f]


def call(body, outs, *operands, scratch=(), space=pltpu.VMEM, vmem=16):
    here = pl.BlockSpec(memory_space=pltpu.VMEM)
    return pl.pallas_call(
        body,
        out_shape=[jax.ShapeDtypeStruct(s, t) for s, t in outs],
        in_specs=[pl.BlockSpec(memory_space=space)] * len(operands),
        out_specs=[here] * len(outs),
        scratch_shapes=list(scratch),
        compiler_params=pltpu.CompilerParams(vmem_limit_bytes=vmem * 1024 * 1024),
    )(*operands)


def exchange(message):
    flat = message.reshape(AF, 1, message.shape[0] // AF * 128)
    flat = lax.all_to_all(flat, "af", split_axis=0, concat_axis=0, tiled=True)
    return flat.reshape(message.shape)


def per_device(recorded, kernel, cutoff):
    tables = jnp.asarray(dft_tables())
    cut = cutoff.reshape(QB, 128)
    kernel = kernel.reshape(FB, 2 * SRCS, RECV)
    message = ((AF * MSG, 128), F32)
    data = ((FB, VB, 2 * SRCS), F32)
    model = ((SAMPLES, 128), F32)
    stat = ((8, 128), F32)
    wide = ((FB, 2 * SRCS, RECV), BF16)

    msg, khi, klo, tables = call(
        first_kernel,
        [message, wide, wide, (tables.shape, BF16)],
        recorded, kernel, tables,
        scratch=[
            pltpu.VMEM(recorded.shape, F32),
            pltpu.VMEM(kernel.shape, F32),
            pltpu.SemaphoreType.DMA((FB + 2,)),
        ],
        space=pltpu.HBM,
        vmem=47,
    )
    msg, s1, stats = call(
        functools.partial(model_kernel, 0, False),
        [message, model, stat],
        exchange(msg), cut, tables,
    )
    msg, q1, stats = call(
        functools.partial(data_kernel, 1),
        [message, data, stat],
        exchange(msg), khi, klo, recorded, stats,
    )
    msg, s2, stats = call(
        functools.partial(model_kernel, 2, False),
        [message, model, stat],
        exchange(msg), cut, tables, stats, s1,
    )
    msg, q2, stats = call(
        functools.partial(data_kernel, 3),
        [message, data, stat],
        exchange(msg), khi, klo, q1, stats,
    )
    msg, stats = call(
        functools.partial(model_kernel, 4, True),
        [((AF * LAST, 128), F32), stat],
        exchange(msg), cut, tables, stats, s1, s2,
    )
    arrived = exchange(msg)
    [stats] = call(stats_kernel, [((VERT * 8, 128), F32)], arrived, stats)
    gathered = lax.all_to_all(stats, "vert", split_axis=0, concat_axis=0, tiled=True)
    out = ((VB, TB, RECV), F32)
    return tuple(
        call(
            last_kernel,
            [out, out, data],
            arrived, gathered, recorded, q1, q2,
            scratch=[pltpu.VMEM((64, 128), F32)],
        )
    )


def solution(mesh):
    in_specs = (P("af", "vert", None), P("af", None, None, None), P())
    out_specs = (P("vert", "af", None), P("vert", "af", None), P("af", "vert", None))
    return jax.shard_map(
        per_device, mesh=mesh, in_specs=in_specs, out_specs=out_specs, check_vma=False
    )
```

```python
import functools
import math

import jax
import jax.numpy as jnp
import numpy as np
from jax import lax
from jax.experimental import pallas as pl
from jax.experimental.pallas import tpu as pltpu
from jax.sharding import PartitionSpec as P

FREQS = 256
SAMPLES = 512
RECV = 512
SRCS = 96
EPSILON = 1e-06
F32 = jnp.float32
BF16 = jnp.bfloat16

AF = 32
VERT = 8
FB = FREQS // AF
VB = 8
QB = RECV // 128
KB = 2 * FB
MSG = KB + 1
TB = SAMPLES // AF
LAST = 3 * TB + 1
CHUNKS = ((0, 2), (2, 2), (4, 2), (6, 2))


def dft_tables():
    times = np.arange(SAMPLES)
    freqs = np.arange(FREQS)
    angles = 2.0 * math.pi / SAMPLES * ((times[:, None] * freqs[None, :]) % SAMPLES)
    scale = 1.0 / math.sqrt(SAMPLES)
    table = np.stack([np.cos(angles), -np.sin(angles)], axis=2) * scale
    table = table.reshape(SAMPLES, 2 * FREQS).astype(np.float32)
    out = []
    for t in (table, np.ascontiguousarray(table.T)):
        hi = t.astype(jnp.bfloat16)
        out += [hi, (t - hi.astype(np.float32)).astype(jnp.bfloat16)]
    return np.stack(out)


def split(x):
    hi = x.astype(BF16)
    return hi, (x - hi.astype(F32)).astype(BF16)


def dot(a, b):
    return lax.dot_general(a, b, (((1,), (0,)), ((), ())), preferred_element_type=F32)


def dot_nt(a, b):
    return lax.dot_general(a, b, (((1,), (1,)), ((), ())), preferred_element_type=F32)


def turned(x, sign):
    return jnp.concatenate([sign * x[:, SRCS:], -sign * x[:, :SRCS]], axis=1)


def kernel_adjoint(u, khi, klo):
    hi, lo = split(jnp.concatenate([u, turned(u, 1.0)], axis=0))
    both = dot(jnp.concatenate([hi, lo], axis=0), khi)
    return both[: 2 * VB] + both[2 * VB :] + dot(hi, klo)


def kernel_forward(x, khi, klo):
    hi, lo = split(x)
    both = dot_nt(jnp.concatenate([hi, lo], axis=0), khi)
    y = both[: 2 * VB] + both[2 * VB :] + dot_nt(hi, klo)
    return y[:VB] + turned(y[VB:], -1.0)


def ratio(a, b):
    return jnp.where(b > 0, a / jnp.where(b > 0, b, 1.0), 0.0)


def arrived_sum(recv, pitch):
    rows = recv[pl.ds(pitch - 1, AF, stride=pitch), :]
    return jnp.broadcast_to(jnp.sum(rows, keepdims=True), (1, 128))


def lane_zero(total):
    lane = lax.broadcasted_iota(jnp.int32, (1, 128), 1)
    return jnp.where(lane == 0, jnp.broadcast_to(total, (1, 128)), 0.0)


def put_spectra(msg, f, z):
    for c in range(2):
        for q in range(QB):
            msg[pl.ds(q * MSG + 2 * f + c, VB, stride=QB * MSG), :] = z[
                c * VB : (c + 1) * VB, q * 128 : (q + 1) * 128
            ]


def put_partial(msg, row, pitch):
    for d in range(AF):
        msg[pl.ds(d * pitch + pitch - 1, 1), :] = row


def halves_kernel(k_hbm, khi_ref, klo_ref, k_buf, sems):
    copies = [
        pltpu.make_async_copy(k_hbm.at[pl.ds(at, n)], k_buf.at[pl.ds(at, n)], sems.at[i])
        for i, (at, n) in enumerate(CHUNKS)
    ]
    for copy in copies:
        copy.start()
    for copy, (at, n) in zip(copies, CHUNKS):
        copy.wait()
        for f in range(at, at + n):
            khi_ref[f], klo_ref[f] = split(k_buf[f])


def first_kernel(u_ref, khi_ref, klo_ref, msg):
    square = jnp.zeros((VB, 2 * SRCS), F32)
    for f in range(FB):
        u = u_ref[f]
        square += u * u
        put_spectra(msg, f, kernel_adjoint(u, khi_ref[f], klo_ref[f]))
    put_partial(msg, lane_zero(jnp.sum(square, keepdims=True)), MSG)


def data_kernel(order, recv, khi_ref, klo_ref, before_ref, stats, msg, q_ref, stats_out):
    total = arrived_sum(recv, MSG)
    stats_out[...] = stats[...]
    stats_out[pl.ds(order, 1), :] = total
    coefficient = ratio(total, stats[pl.ds(order - 1, 1), :])[:, :1]
    square = jnp.zeros((VB, 2 * SRCS), F32)
    steps = []
    for f in range(FB):
        x = jnp.concatenate(
            [
                jnp.concatenate(
                    [
                        recv[pl.ds(q * MSG + 2 * f + c, VB, stride=QB * MSG), :]
                        for q in range(QB)
                    ],
                    axis=1,
                )
                for c in range(2)
            ],
            axis=0,
        )
        u = kernel_forward(x, khi_ref[f], klo_ref[f]) - coefficient * before_ref[f]
        q_ref[f] = u
        square += u * u
        steps.append(u)
    for f in range(FB):
        put_spectra(msg, f, kernel_adjoint(steps[f], khi_ref[f], klo_ref[f]))
    put_partial(msg, lane_zero(jnp.sum(square, keepdims=True)), MSG)


def table_apply(table_ref, at, x):
    hi, lo = split(x)
    both = dot(table_ref[at], jnp.concatenate([hi, lo], axis=1))
    return both[:, :128] + both[:, 128:] + dot(table_ref[at + 1], hi)


def model_kernel(order, last, *refs):
    refs = list(refs)
    recv, cut_ref, table_ref = refs[:3]
    refs = refs[3:]
    if order > 0:
        stats = refs.pop(0)
        earlier = [refs.pop(0) for _ in range(order // 2)]
    total = arrived_sum(recv, MSG)
    spectra = jnp.concatenate([recv[pl.ds(p * MSG, KB), :] for p in range(AF)], axis=0)
    s = table_apply(table_ref, 0, spectra)
    if order > 0:
        s = s - ratio(total, stats[pl.ds(order - 1, 1), :]) * earlier[-1][...]
    cut = cut_ref[pl.ds(lax.rem(lax.axis_index("af"), QB), 1), :]
    keep = lax.broadcasted_iota(jnp.int32, (SAMPLES, 128), 0) < cut
    s = jnp.where(keep, s, 0.0)
    partial = jnp.sum(s * s, axis=0, keepdims=True)
    if last:
        msg, stats_out = refs
    else:
        msg, s_ref, stats_out = refs
        s_ref[...] = s
    stats_out[...] = stats[...] if order > 0 else jnp.zeros((8, 128), F32)
    stats_out[pl.ds(order, 1), :] = total
    if last:
        for j, value in enumerate([e[...] for e in earlier] + [s]):
            for p in range(AF):
                msg[pl.ds(p * LAST + j * TB, TB), :] = value[p * TB : (p + 1) * TB]
        put_partial(msg, partial, LAST)
    else:
        out = table_apply(table_ref, 2, s)
        for p in range(AF):
            msg[pl.ds(p * MSG, KB), :] = out[p * KB : (p + 1) * KB]
        put_partial(msg, partial, MSG)


def stats_kernel(recv, stats, out):
    total = arrived_sum(recv, LAST)
    row = lax.broadcasted_iota(jnp.int32, (8, 128), 0)
    mine = jnp.where(row == 5, total, stats[...])
    for g in range(VERT):
        out[pl.ds(8 * g, 8), :] = mine


def last_kernel(recv, gathered, q0_ref, q1_ref, q2_ref, sol_ref, dir_ref, left_ref, rows):
    n0, m1, n1, m2, n2, m3 = [gathered[pl.ds(j, VERT, stride=8), :] for j in range(6)]

    def norm(x):
        return jnp.sqrt(jnp.sum(x, axis=0, keepdims=True) + EPSILON)

    theta, kappa, lam, mu = ratio(m1, n0), ratio(n1, m1), ratio(m2, n1), ratio(n2, m2)
    beta0 = norm(n0)
    alpha1 = norm(m1 / (beta0 * beta0))
    e = 1.0 / (beta0 * alpha1)
    d = e * theta - alpha1 / beta0
    beta1 = norm(e * e * n1 + d * d * n0)
    f1 = e / beta1
    f0 = d / beta1
    h = f1 * kappa + f0 - beta1 * e
    alpha2 = norm(f1 * f1 * m2 + h * h * m1)
    g2 = f1 / alpha2
    g1 = h / alpha2
    rho1 = jnp.sqrt(alpha1 * alpha1 + beta1 * beta1)
    cos1, sin1 = alpha1 / rho1, beta1 / rho1
    theta1 = sin1 * alpha2
    rhobar = -cos1 * alpha2
    phi1, phibar = cos1 * beta0, sin1 * beta0
    w2 = g2
    w1 = g1 - theta1 / rho1 * e
    c2 = g2
    c1 = g2 * lam + g1 - alpha2 * f1
    c0 = g1 * theta - alpha2 * f0
    beta2 = norm(c2 * c2 * n2 + c1 * c1 * n1 + c0 * c0 * n0)
    c2, c1, c0 = c2 / beta2, c1 / beta2, c0 / beta2
    z3 = c2
    z2 = c2 * mu + c1 - beta2 * g2
    z1 = c1 * kappa + c0 - beta2 * g1
    alpha3 = norm(z3 * z3 * m3 + z2 * z2 * m2 + z1 * z1 * m1)
    rho2 = jnp.sqrt(rhobar * rhobar + beta2 * beta2)
    cos2, sin2 = rhobar / rho2, beta2 / rho2
    step2 = cos2 * phibar / rho2
    turn2 = sin2 * alpha3 / rho2
    x1 = phi1 / rho1 * e + step2 * w1
    x2 = step2 * w2
    y1 = z1 / alpha3 - turn2 * w1
    y2 = z2 / alpha3 - turn2 * w2
    y3 = z3 / alpha3
    for j, value in enumerate((x1, x2, y1, y2, y3, c0, c1, c2)):
        rows[pl.ds(8 * j, 8), :] = jnp.broadcast_to(value, (VERT, 128))
    group = lax.axis_index("vert")
    x1, x2, y1, y2, y3, c0, c1, c2 = [rows[pl.ds(8 * j + group, 1), :] for j in range(8)]
    for v in range(VB):
        for q in range(QB):
            at = (v * QB + q) * LAST
            s1, s2, s3 = [recv[pl.ds(at + j * TB, TB), :] for j in range(3)]
            sol_ref[v, :, q * 128 : (q + 1) * 128] = x1 * s1 + x2 * s2
            dir_ref[v, :, q * 128 : (q + 1) * 128] = y1 * s1 + y2 * s2 + y3 * s3
    c0, c1, c2 = c0[:, :1], c1[:, :1], c2[:, :1]
    for f in range(FB):
        left_ref[f] = c0 * q0_ref[f] + c1 * q1_ref[f] + c2 * q2_ref[f]


def call(body, outs, *operands, scratch=(), space=pltpu.VMEM, vmem=16):
    here = pl.BlockSpec(memory_space=pltpu.VMEM)
    return pl.pallas_call(
        body,
        out_shape=[jax.ShapeDtypeStruct(s, t) for s, t in outs],
        in_specs=[pl.BlockSpec(memory_space=space)] * len(operands),
        out_specs=[here] * len(outs),
        scratch_shapes=list(scratch),
        compiler_params=pltpu.CompilerParams(vmem_limit_bytes=vmem * 1024 * 1024),
    )(*operands)


def exchange(message):
    flat = message.reshape(AF, 1, message.shape[0] // AF * 128)
    flat = lax.all_to_all(flat, "af", split_axis=0, concat_axis=0, tiled=True)
    return flat.reshape(message.shape)


def per_device(recorded, kernel, cutoff):
    tables = jnp.asarray(dft_tables())
    cut = cutoff.reshape(QB, 128)
    kernel = kernel.reshape(FB, 2 * SRCS, RECV)
    message = ((AF * MSG, 128), F32)
    data = ((FB, VB, 2 * SRCS), F32)
    model = ((SAMPLES, 128), F32)
    stat = ((8, 128), F32)
    wide = ((FB, 2 * SRCS, RECV), BF16)

    khi, klo = call(
        halves_kernel,
        [wide, wide],
        kernel,
        scratch=[pltpu.VMEM(kernel.shape, F32), pltpu.SemaphoreType.DMA((len(CHUNKS),))],
        space=pltpu.HBM,
        vmem=49,
    )
    [msg] = call(first_kernel, [message], recorded, khi, klo)
    msg, s1, stats = call(
        functools.partial(model_kernel, 0, False),
        [message, model, stat],
        exchange(msg), cut, tables,
    )
    msg, q1, stats = call(
        functools.partial(data_kernel, 1),
        [message, data, stat],
        exchange(msg), khi, klo, recorded, stats,
    )
    msg, s2, stats = call(
        functools.partial(model_kernel, 2, False),
        [message, model, stat],
        exchange(msg), cut, tables, stats, s1,
    )
    msg, q2, stats = call(
        functools.partial(data_kernel, 3),
        [message, data, stat],
        exchange(msg), khi, klo, q1, stats,
    )
    msg, stats = call(
        functools.partial(model_kernel, 4, True),
        [((AF * LAST, 128), F32), stat],
        exchange(msg), cut, tables, stats, s1, s2,
    )
    arrived = exchange(msg)
    [stats] = call(stats_kernel, [((VERT * 8, 128), F32)], arrived, stats)
    gathered = lax.all_to_all(stats, "vert", split_axis=0, concat_axis=0, tiled=True)
    out = ((VB, TB, RECV), F32)
    return tuple(
        call(
            last_kernel,
            [out, out, data],
            arrived, gathered, recorded, q1, q2,
            scratch=[pltpu.VMEM((64, 128), F32)],
        )
    )


def solution(mesh):
    in_specs = (P("af", "vert", None), P("af", None, None, None), P())
    out_specs = (P("vert", "af", None), P("vert", "af", None), P("af", "vert", None))
    return jax.shard_map(
        per_device, mesh=mesh, in_specs=in_specs, out_specs=out_specs, check_vma=False
    )
```

```python
import functools
import math

import jax
import jax.numpy as jnp
import numpy as np
from jax import lax
from jax.experimental import pallas as pl
from jax.experimental.pallas import tpu as pltpu
from jax.sharding import PartitionSpec as P

FREQS = 256
SAMPLES = 512
RECV = 512
SRCS = 96
EPSILON = 1e-06
F32 = jnp.float32
BF16 = jnp.bfloat16

AF = 32
VERT = 8
FB = FREQS // AF
VB = 8
QB = RECV // 128
KB = 2 * FB
MSG = KB + 1
TB = SAMPLES // AF
LAST = 3 * TB + 1
CHUNKS = ((0, 2), (2, 2), (4, 2), (6, 2))


def dft_tables():
    times = np.arange(SAMPLES)
    freqs = np.arange(FREQS)
    angles = 2.0 * math.pi / SAMPLES * ((times[:, None] * freqs[None, :]) % SAMPLES)
    scale = 1.0 / math.sqrt(SAMPLES)
    table = np.stack([np.cos(angles), -np.sin(angles)], axis=2) * scale
    table = table.reshape(SAMPLES, 2 * FREQS).astype(np.float32)
    out = []
    for t in (table, np.ascontiguousarray(table.T)):
        hi = t.astype(jnp.bfloat16)
        out += [hi, (t - hi.astype(np.float32)).astype(jnp.bfloat16)]
    return np.stack(out)


def split(x):
    hi = x.astype(BF16)
    return hi, (x - hi.astype(F32)).astype(BF16)


def dot(a, b):
    return lax.dot_general(a, b, (((1,), (0,)), ((), ())), preferred_element_type=F32)


def dot_nt(a, b):
    return lax.dot_general(a, b, (((1,), (1,)), ((), ())), preferred_element_type=F32)


def turned(x, sign):
    return jnp.concatenate([sign * x[:, SRCS:], -sign * x[:, :SRCS]], axis=1)


def kernel_adjoint(u, khi, klo):
    hi, lo = split(jnp.concatenate([u, turned(u, 1.0)], axis=0))
    both = dot(jnp.concatenate([hi, lo], axis=0), khi)
    return both[: 2 * VB] + both[2 * VB :] + dot(hi, klo)


def kernel_forward(x, khi, klo):
    hi, lo = split(x)
    both = dot_nt(jnp.concatenate([hi, lo], axis=0), khi)
    y = both[: 2 * VB] + both[2 * VB :] + dot_nt(hi, klo)
    return y[:VB] + turned(y[VB:], -1.0)


def ratio(a, b):
    return jnp.where(b > 0, a / jnp.where(b > 0, b, 1.0), 0.0)


def arrived_sum(recv, pitch):
    rows = recv[pl.ds(pitch - 1, AF, stride=pitch), :]
    return jnp.broadcast_to(jnp.sum(rows, keepdims=True), (1, 128))


def lane_zero(total):
    lane = lax.broadcasted_iota(jnp.int32, (1, 128), 1)
    return jnp.where(lane == 0, jnp.broadcast_to(total, (1, 128)), 0.0)


def put_spectra(msg, f, z):
    for c in range(2):
        for q in range(QB):
            msg[pl.ds(q * MSG + 2 * f + c, VB, stride=QB * MSG), :] = z[
                c * VB : (c + 1) * VB, q * 128 : (q + 1) * 128
            ]


def put_partial(msg, row, pitch):
    for d in range(AF):
        msg[pl.ds(d * pitch + pitch - 1, 1), :] = row


def halves_kernel(k_hbm, khi_ref, klo_ref, k_buf, sems):
    copies = [
        pltpu.make_async_copy(k_hbm.at[pl.ds(at, n)], k_buf.at[pl.ds(at, n)], sems.at[i])
        for i, (at, n) in enumerate(CHUNKS)
    ]
    for copy in copies:
        copy.start()
    for copy, (at, n) in zip(copies, CHUNKS):
        copy.wait()
        for f in range(at, at + n):
            khi_ref[f], klo_ref[f] = split(k_buf[f])


def first_kernel(u_ref, khi_ref, klo_ref, msg):
    square = jnp.zeros((VB, 2 * SRCS), F32)
    for f in range(FB):
        u = u_ref[f]
        square += u * u
        put_spectra(msg, f, kernel_adjoint(u, khi_ref[f], klo_ref[f]))
    put_partial(msg, lane_zero(jnp.sum(square, keepdims=True)), MSG)


def data_kernel(order, recv, khi_ref, klo_ref, before_ref, stats, msg, q_ref, stats_out):
    total = arrived_sum(recv, MSG)
    stats_out[...] = stats[...]
    stats_out[pl.ds(order, 1), :] = total
    coefficient = ratio(total, stats[pl.ds(order - 1, 1), :])[:, :1]
    square = jnp.zeros((VB, 2 * SRCS), F32)
    steps = []
    for f in range(FB):
        x = jnp.concatenate(
            [
                jnp.concatenate(
                    [
                        recv[pl.ds(q * MSG + 2 * f + c, VB, stride=QB * MSG), :]
                        for q in range(QB)
                    ],
                    axis=1,
                )
                for c in range(2)
            ],
            axis=0,
        )
        u = kernel_forward(x, khi_ref[f], klo_ref[f]) - coefficient * before_ref[f]
        q_ref[f] = u
        square += u * u
        steps.append(u)
    for f in range(FB):
        put_spectra(msg, f, kernel_adjoint(steps[f], khi_ref[f], klo_ref[f]))
    put_partial(msg, lane_zero(jnp.sum(square, keepdims=True)), MSG)


def table_apply(table_ref, at, x):
    hi, lo = split(x)
    both = dot(table_ref[at], jnp.concatenate([hi, lo], axis=1))
    return both[:, :128] + both[:, 128:] + dot(table_ref[at + 1], hi)


def model_kernel(order, last, *refs):
    refs = list(refs)
    recv, cut_ref, table_ref = refs[:3]
    refs = refs[3:]
    if order > 0:
        stats = refs.pop(0)
        earlier = [refs.pop(0) for _ in range(order // 2)]
    total = arrived_sum(recv, MSG)
    spectra = jnp.concatenate([recv[pl.ds(p * MSG, KB), :] for p in range(AF)], axis=0)
    s = table_apply(table_ref, 0, spectra)
    if order > 0:
        s = s - ratio(total, stats[pl.ds(order - 1, 1), :]) * earlier[-1][...]
    cut = cut_ref[pl.ds(lax.rem(lax.axis_index("af"), QB), 1), :]
    keep = lax.broadcasted_iota(jnp.int32, (SAMPLES, 128), 0) < cut
    s = jnp.where(keep, s, 0.0)
    partial = jnp.sum(s * s, axis=0, keepdims=True)
    if last:
        msg, stats_out = refs
    else:
        msg, s_ref, stats_out = refs
        s_ref[...] = s
    stats_out[...] = stats[...] if order > 0 else jnp.zeros((8, 128), F32)
    stats_out[pl.ds(order, 1), :] = total
    if last:
        for j, value in enumerate([e[...] for e in earlier] + [s]):
            for p in range(AF):
                msg[pl.ds(p * LAST + j * TB, TB), :] = value[p * TB : (p + 1) * TB]
        put_partial(msg, partial, LAST)
    else:
        out = table_apply(table_ref, 2, s)
        for p in range(AF):
            msg[pl.ds(p * MSG, KB), :] = out[p * KB : (p + 1) * KB]
        put_partial(msg, partial, MSG)


def stats_kernel(recv, stats, out):
    total = arrived_sum(recv, LAST)
    row = lax.broadcasted_iota(jnp.int32, (8, 128), 0)
    out[...] = jnp.where(row == 5, total, stats[...])


def pair_kernel(mine, other, out):
    out[pl.ds(0, 8), :] = mine[...]
    out[pl.ds(8, 8), :] = other[...]


def last_kernel(recv, g0, g1, g2, g3, q0_ref, q1_ref, q2_ref, sol_ref, dir_ref, left_ref, rows):
    gathered = (g0, g1, g2, g3)
    n0, m1, n1, m2, n2, m3 = [
        jnp.concatenate([g[pl.ds(8 * c + j, 1), :] for g in gathered for c in range(2)], axis=0)
        for j in range(6)
    ]

    def norm(x):
        return jnp.sqrt(jnp.sum(x, axis=0, keepdims=True) + EPSILON)

    theta, kappa, lam, mu = ratio(m1, n0), ratio(n1, m1), ratio(m2, n1), ratio(n2, m2)
    beta0 = norm(n0)
    alpha1 = norm(m1 / (beta0 * beta0))
    e = 1.0 / (beta0 * alpha1)
    d = e * theta - alpha1 / beta0
    beta1 = norm(e * e * n1 + d * d * n0)
    f1 = e / beta1
    f0 = d / beta1
    h = f1 * kappa + f0 - beta1 * e
    alpha2 = norm(f1 * f1 * m2 + h * h * m1)
    g2 = f1 / alpha2
    g1 = h / alpha2
    rho1 = jnp.sqrt(alpha1 * alpha1 + beta1 * beta1)
    cos1, sin1 = alpha1 / rho1, beta1 / rho1
    theta1 = sin1 * alpha2
    rhobar = -cos1 * alpha2
    phi1, phibar = cos1 * beta0, sin1 * beta0
    w2 = g2
    w1 = g1 - theta1 / rho1 * e
    c2 = g2
    c1 = g2 * lam + g1 - alpha2 * f1
    c0 = g1 * theta - alpha2 * f0
    beta2 = norm(c2 * c2 * n2 + c1 * c1 * n1 + c0 * c0 * n0)
    c2, c1, c0 = c2 / beta2, c1 / beta2, c0 / beta2
    z3 = c2
    z2 = c2 * mu + c1 - beta2 * g2
    z1 = c1 * kappa + c0 - beta2 * g1
    alpha3 = norm(z3 * z3 * m3 + z2 * z2 * m2 + z1 * z1 * m1)
    rho2 = jnp.sqrt(rhobar * rhobar + beta2 * beta2)
    cos2, sin2 = rhobar / rho2, beta2 / rho2
    step2 = cos2 * phibar / rho2
    turn2 = sin2 * alpha3 / rho2
    x1 = phi1 / rho1 * e + step2 * w1
    x2 = step2 * w2
    y1 = z1 / alpha3 - turn2 * w1
    y2 = z2 / alpha3 - turn2 * w2
    y3 = z3 / alpha3
    for j, value in enumerate((x1, x2, y1, y2, y3, c0, c1, c2)):
        rows[pl.ds(8 * j, 8), :] = jnp.broadcast_to(value, (VERT, 128))
    group = 0
    x1, x2, y1, y2, y3, c0, c1, c2 = [rows[pl.ds(8 * j + group, 1), :] for j in range(8)]
    for v in range(VB):
        for q in range(QB):
            at = (v * QB + q) * LAST
            s1, s2, s3 = [recv[pl.ds(at + j * TB, TB), :] for j in range(3)]
            sol_ref[v, :, q * 128 : (q + 1) * 128] = x1 * s1 + x2 * s2
            dir_ref[v, :, q * 128 : (q + 1) * 128] = y1 * s1 + y2 * s2 + y3 * s3
    c0, c1, c2 = c0[:, :1], c1[:, :1], c2[:, :1]
    for f in range(FB):
        left_ref[f] = c0 * q0_ref[f] + c1 * q1_ref[f] + c2 * q2_ref[f]


def call(body, outs, *operands, scratch=(), space=pltpu.VMEM, vmem=16):
    here = pl.BlockSpec(memory_space=pltpu.VMEM)
    return pl.pallas_call(
        body,
        out_shape=[jax.ShapeDtypeStruct(s, t) for s, t in outs],
        in_specs=[pl.BlockSpec(memory_space=space)] * len(operands),
        out_specs=[here] * len(outs),
        scratch_shapes=list(scratch),
        compiler_params=pltpu.CompilerParams(vmem_limit_bytes=vmem * 1024 * 1024),
    )(*operands)


def exchange(message):
    flat = message.reshape(AF, 1, message.shape[0] // AF * 128)
    flat = lax.all_to_all(flat, "af", split_axis=0, concat_axis=0, tiled=True)
    return flat.reshape(message.shape)


def per_device(recorded, kernel, cutoff):
    tables = jnp.asarray(dft_tables())
    cut = cutoff.reshape(QB, 128)
    kernel = kernel.reshape(FB, 2 * SRCS, RECV)
    message = ((AF * MSG, 128), F32)
    data = ((FB, VB, 2 * SRCS), F32)
    model = ((SAMPLES, 128), F32)
    stat = ((8, 128), F32)
    wide = ((FB, 2 * SRCS, RECV), BF16)

    khi, klo = call(
        halves_kernel,
        [wide, wide],
        kernel,
        scratch=[pltpu.VMEM(kernel.shape, F32), pltpu.SemaphoreType.DMA((len(CHUNKS),))],
        space=pltpu.HBM,
        vmem=49,
    )
    [msg] = call(first_kernel, [message], recorded, khi, klo)
    msg, s1, stats = call(
        functools.partial(model_kernel, 0, False),
        [message, model, stat],
        exchange(msg), cut, tables,
    )
    msg, q1, stats = call(
        functools.partial(data_kernel, 1),
        [message, data, stat],
        exchange(msg), khi, klo, recorded, stats,
    )
    msg, s2, stats = call(
        functools.partial(model_kernel, 2, False),
        [message, model, stat],
        exchange(msg), cut, tables, stats, s1,
    )
    msg, q2, stats = call(
        functools.partial(data_kernel, 3),
        [message, data, stat],
        exchange(msg), khi, klo, q1, stats,
    )
    msg, stats = call(
        functools.partial(model_kernel, 4, True),
        [((AF * LAST, 128), F32), stat],
        exchange(msg), cut, tables, stats, s1, s2,
    )
    arrived = exchange(msg)
    [stats] = call(stats_kernel, [stat], arrived, stats)
    [pair] = call(pair_kernel, [((16, 128), F32)], stats, lax.ppermute(stats, "vert", [(i, i ^ 1) for i in range(VERT)]))
    gathered = [pair] + [lax.ppermute(pair, "vert", [(i, i ^ (2 * d)) for i in range(VERT)]) for d in (1, 2, 3)]
    out = ((VB, TB, RECV), F32)
    return tuple(
        call(
            last_kernel,
            [out, out, data],
            arrived, *gathered, recorded, q1, q2,
            scratch=[pltpu.VMEM((64, 128), F32)],
        )
    )


def solution(mesh):
    in_specs = (P("af", "vert", None), P("af", None, None, None), P())
    out_specs = (P("vert", "af", None), P("vert", "af", None), P("af", "vert", None))
    return jax.shard_map(
        per_device, mesh=mesh, in_specs=in_specs, out_specs=out_specs, check_vma=False
    )
```

```python
import functools
import math

import jax
import jax.numpy as jnp
import numpy as np
from jax import lax
from jax.experimental import pallas as pl
from jax.experimental.pallas import tpu as pltpu
from jax.sharding import PartitionSpec as P

FREQS = 256
SAMPLES = 512
RECV = 512
SRCS = 96
EPSILON = 1e-06
F32 = jnp.float32
BF16 = jnp.bfloat16

AF = 32
VERT = 8
FB = FREQS // AF
VB = 8
QB = RECV // 128
KB = 2 * FB
MSG = KB + 1
TB = SAMPLES // AF
LAST = 3 * TB + 1
CHUNKS = ((0, 2), (2, 2), (4, 2), (6, 2))


def dft_tables():
    times = np.arange(SAMPLES)
    freqs = np.arange(FREQS)
    angles = 2.0 * math.pi / SAMPLES * ((times[:, None] * freqs[None, :]) % SAMPLES)
    scale = 1.0 / math.sqrt(SAMPLES)
    table = np.stack([np.cos(angles), -np.sin(angles)], axis=2) * scale
    table = table.reshape(SAMPLES, 2 * FREQS).astype(np.float32)
    out = []
    for t in (table, np.ascontiguousarray(table.T)):
        hi = t.astype(jnp.bfloat16)
        out += [hi, (t - hi.astype(np.float32)).astype(jnp.bfloat16)]
    return np.stack(out)


def split(x):
    hi = x.astype(BF16)
    return hi, (x - hi.astype(F32)).astype(BF16)


def dot(a, b):
    return lax.dot_general(a, b, (((1,), (0,)), ((), ())), preferred_element_type=F32)


def dot_nt(a, b):
    return lax.dot_general(a, b, (((1,), (1,)), ((), ())), preferred_element_type=F32)


def turned(x, sign):
    return jnp.concatenate([sign * x[:, SRCS:], -sign * x[:, :SRCS]], axis=1)


def kernel_adjoint(u, khi, klo):
    hi, lo = split(jnp.concatenate([u, turned(u, 1.0)], axis=0))
    both = dot(jnp.concatenate([hi, lo], axis=0), khi)
    return both[: 2 * VB] + both[2 * VB :] + dot(hi, klo)


def kernel_forward(x, khi, klo, product):
    hi, lo = split(x)
    both = product(jnp.concatenate([hi, lo], axis=0), khi)
    y = both[: 2 * VB] + both[2 * VB :] + product(hi, klo)
    return y[:VB] + turned(y[VB:], -1.0)


def on_core(core):
    return lax.rem(lax.axis_index("vert"), 2) == core


def ratio(a, b):
    return jnp.where(b > 0, a / jnp.where(b > 0, b, 1.0), 0.0)


def arrived_sum(recv, pitch):
    rows = recv[pl.ds(pitch - 1, AF, stride=pitch), :]
    return jnp.broadcast_to(jnp.sum(rows, keepdims=True), (1, 128))


def lane_zero(total):
    lane = lax.broadcasted_iota(jnp.int32, (1, 128), 1)
    return jnp.where(lane == 0, jnp.broadcast_to(total, (1, 128)), 0.0)


def put_spectra(msg, f, z):
    for c in range(2):
        for q in range(QB):
            msg[pl.ds(q * MSG + 2 * f + c, VB, stride=QB * MSG), :] = z[
                c * VB : (c + 1) * VB, q * 128 : (q + 1) * 128
            ]


def put_partial(msg, row, pitch):
    for d in range(AF):
        msg[pl.ds(d * pitch + pitch - 1, 1), :] = row


def halves_kernel(k_hbm, khi_ref, klo_ref, k_buf, sems):
    copies = [
        pltpu.make_async_copy(k_hbm.at[pl.ds(at, n)], k_buf.at[pl.ds(at, n)], sems.at[i])
        for i, (at, n) in enumerate(CHUNKS)
    ]
    for copy in copies:
        copy.start()
    for copy, (at, n) in zip(copies, CHUNKS):
        copy.wait()
        for f in range(at, at + n):
            khi_ref[f], klo_ref[f] = split(k_buf[f])


def first_kernel(u_ref, khi_ref, klo_ref, msg, thi_ref, tlo_ref):
    square = jnp.zeros((VB, 2 * SRCS), F32)
    for f in range(FB):
        u = u_ref[f]
        square += u * u
        put_spectra(msg, f, kernel_adjoint(u, khi_ref[f], klo_ref[f]))
    put_partial(msg, lane_zero(jnp.sum(square, keepdims=True)), MSG)

    @pl.when(on_core(0))
    def _():
        for f in range(FB):
            thi_ref[f] = khi_ref[f].T
            tlo_ref[f] = klo_ref[f].T


def data_kernel(
    order, recv, khi_ref, klo_ref, thi_ref, tlo_ref, before_ref, stats, msg, q_ref, stats_out
):
    total = arrived_sum(recv, MSG)
    stats_out[...] = stats[...]
    stats_out[pl.ds(order, 1), :] = total
    coefficient = ratio(total, stats[pl.ds(order - 1, 1), :])[:, :1]

    def step(hi_ref, lo_ref, product):
        square = jnp.zeros((VB, 2 * SRCS), F32)
        steps = []
        for f in range(FB):
            x = jnp.concatenate(
                [
                    jnp.concatenate(
                        [
                            recv[pl.ds(q * MSG + 2 * f + c, VB, stride=QB * MSG), :]
                            for q in range(QB)
                        ],
                        axis=1,
                    )
                    for c in range(2)
                ],
                axis=0,
            )
            u = kernel_forward(x, hi_ref[f], lo_ref[f], product) - coefficient * before_ref[f]
            q_ref[f] = u
            square += u * u
            steps.append(u)
        for f in range(FB):
            put_spectra(msg, f, kernel_adjoint(steps[f], khi_ref[f], klo_ref[f]))
        put_partial(msg, lane_zero(jnp.sum(square, keepdims=True)), MSG)

    pl.when(on_core(0))(lambda: step(thi_ref, tlo_ref, dot))
    pl.when(on_core(1))(lambda: step(khi_ref, klo_ref, dot_nt))


def table_apply(table_ref, at, x):
    hi, lo = split(x)
    both = dot(table_ref[at], jnp.concatenate([hi, lo], axis=1))
    return both[:, :128] + both[:, 128:] + dot(table_ref[at + 1], hi)


def model_kernel(order, last, *refs):
    refs = list(refs)
    recv, cut_ref, table_ref = refs[:3]
    refs = refs[3:]
    if order > 0:
        stats = refs.pop(0)
        earlier = [refs.pop(0) for _ in range(order // 2)]
    total = arrived_sum(recv, MSG)
    spectra = jnp.concatenate([recv[pl.ds(p * MSG, KB), :] for p in range(AF)], axis=0)
    s = table_apply(table_ref, 0, spectra)
    if order > 0:
        s = s - ratio(total, stats[pl.ds(order - 1, 1), :]) * earlier[-1][...]
    cut = cut_ref[pl.ds(lax.rem(lax.axis_index("af"), QB), 1), :]
    keep = lax.broadcasted_iota(jnp.int32, (SAMPLES, 128), 0) < cut
    s = jnp.where(keep, s, 0.0)
    partial = jnp.sum(s * s, axis=0, keepdims=True)
    if last:
        msg, stats_out = refs
    else:
        msg, s_ref, stats_out = refs
        s_ref[...] = s
    stats_out[...] = stats[...] if order > 0 else jnp.zeros((8, 128), F32)
    stats_out[pl.ds(order, 1), :] = total
    if last:
        for j, value in enumerate([e[...] for e in earlier] + [s]):
            for p in range(AF):
                msg[pl.ds(p * LAST + j * TB, TB), :] = value[p * TB : (p + 1) * TB]
        put_partial(msg, partial, LAST)
    else:
        out = table_apply(table_ref, 2, s)
        for p in range(AF):
            msg[pl.ds(p * MSG, KB), :] = out[p * KB : (p + 1) * KB]
        put_partial(msg, partial, MSG)


def stats_kernel(recv, stats, out):
    total = arrived_sum(recv, LAST)
    row = lax.broadcasted_iota(jnp.int32, (8, 128), 0)
    out[...] = jnp.where(row == 5, total, stats[...])


def pair_kernel(mine, other, out):
    out[pl.ds(0, 8), :] = mine[...]
    out[pl.ds(8, 8), :] = other[...]


def last_kernel(recv, g0, g1, g2, g3, q0_ref, q1_ref, q2_ref, sol_ref, dir_ref, left_ref, rows):
    gathered = (g0, g1, g2, g3)
    n0, m1, n1, m2, n2, m3 = [
        jnp.concatenate([g[pl.ds(8 * c + j, 1), :] for g in gathered for c in range(2)], axis=0)
        for j in range(6)
    ]

    def norm(x):
        return jnp.sqrt(jnp.sum(x, axis=0, keepdims=True) + EPSILON)

    theta, kappa, lam, mu = ratio(m1, n0), ratio(n1, m1), ratio(m2, n1), ratio(n2, m2)
    beta0 = norm(n0)
    alpha1 = norm(m1 / (beta0 * beta0))
    e = 1.0 / (beta0 * alpha1)
    d = e * theta - alpha1 / beta0
    beta1 = norm(e * e * n1 + d * d * n0)
    f1 = e / beta1
    f0 = d / beta1
    h = f1 * kappa + f0 - beta1 * e
    alpha2 = norm(f1 * f1 * m2 + h * h * m1)
    g2 = f1 / alpha2
    g1 = h / alpha2
    rho1 = jnp.sqrt(alpha1 * alpha1 + beta1 * beta1)
    cos1, sin1 = alpha1 / rho1, beta1 / rho1
    theta1 = sin1 * alpha2
    rhobar = -cos1 * alpha2
    phi1, phibar = cos1 * beta0, sin1 * beta0
    w2 = g2
    w1 = g1 - theta1 / rho1 * e
    c2 = g2
    c1 = g2 * lam + g1 - alpha2 * f1
    c0 = g1 * theta - alpha2 * f0
    beta2 = norm(c2 * c2 * n2 + c1 * c1 * n1 + c0 * c0 * n0)
    c2, c1, c0 = c2 / beta2, c1 / beta2, c0 / beta2
    z3 = c2
    z2 = c2 * mu + c1 - beta2 * g2
    z1 = c1 * kappa + c0 - beta2 * g1
    alpha3 = norm(z3 * z3 * m3 + z2 * z2 * m2 + z1 * z1 * m1)
    rho2 = jnp.sqrt(rhobar * rhobar + beta2 * beta2)
    cos2, sin2 = rhobar / rho2, beta2 / rho2
    step2 = cos2 * phibar / rho2
    turn2 = sin2 * alpha3 / rho2
    x1 = phi1 / rho1 * e + step2 * w1
    x2 = step2 * w2
    y1 = z1 / alpha3 - turn2 * w1
    y2 = z2 / alpha3 - turn2 * w2
    y3 = z3 / alpha3
    for j, value in enumerate((x1, x2, y1, y2, y3, c0, c1, c2)):
        rows[pl.ds(8 * j, 8), :] = jnp.broadcast_to(value, (VERT, 128))
    group = 0
    x1, x2, y1, y2, y3, c0, c1, c2 = [rows[pl.ds(8 * j + group, 1), :] for j in range(8)]
    for v in range(VB):
        for q in range(QB):
            at = (v * QB + q) * LAST
            s1, s2, s3 = [recv[pl.ds(at + j * TB, TB), :] for j in range(3)]
            sol_ref[v, :, q * 128 : (q + 1) * 128] = x1 * s1 + x2 * s2
            dir_ref[v, :, q * 128 : (q + 1) * 128] = y1 * s1 + y2 * s2 + y3 * s3
    c0, c1, c2 = c0[:, :1], c1[:, :1], c2[:, :1]
    for f in range(FB):
        left_ref[f] = c0 * q0_ref[f] + c1 * q1_ref[f] + c2 * q2_ref[f]


def call(body, outs, *operands, scratch=(), space=pltpu.VMEM, vmem=16):
    here = pl.BlockSpec(memory_space=pltpu.VMEM)
    return pl.pallas_call(
        body,
        out_shape=[jax.ShapeDtypeStruct(s, t) for s, t in outs],
        in_specs=[pl.BlockSpec(memory_space=space)] * len(operands),
        out_specs=[here] * len(outs),
        scratch_shapes=list(scratch),
        compiler_params=pltpu.CompilerParams(vmem_limit_bytes=vmem * 1024 * 1024),
    )(*operands)


def exchange(message):
    flat = message.reshape(AF, 1, message.shape[0] // AF * 128)
    flat = lax.all_to_all(flat, "af", split_axis=0, concat_axis=0, tiled=True)
    return flat.reshape(message.shape)


def per_device(recorded, kernel, cutoff):
    tables = jnp.asarray(dft_tables())
    cut = cutoff.reshape(QB, 128)
    kernel = kernel.reshape(FB, 2 * SRCS, RECV)
    message = ((AF * MSG, 128), F32)
    data = ((FB, VB, 2 * SRCS), F32)
    model = ((SAMPLES, 128), F32)
    stat = ((8, 128), F32)
    wide = ((FB, 2 * SRCS, RECV), BF16)

    khi, klo = call(
        halves_kernel,
        [wide, wide],
        kernel,
        scratch=[pltpu.VMEM(kernel.shape, F32), pltpu.SemaphoreType.DMA((len(CHUNKS),))],
        space=pltpu.HBM,
        vmem=49,
    )
    turned_halves = ((FB, RECV, 2 * SRCS), BF16)
    msg, thi, tlo = call(
        first_kernel, [message, turned_halves, turned_halves], recorded, khi, klo
    )
    msg, s1, stats = call(
        functools.partial(model_kernel, 0, False),
        [message, model, stat],
        exchange(msg), cut, tables,
    )
    msg, q1, stats = call(
        functools.partial(data_kernel, 1),
        [message, data, stat],
        exchange(msg), khi, klo, thi, tlo, recorded, stats,
    )
    msg, s2, stats = call(
        functools.partial(model_kernel, 2, False),
        [message, model, stat],
        exchange(msg), cut, tables, stats, s1,
    )
    msg, q2, stats = call(
        functools.partial(data_kernel, 3),
        [message, data, stat],
        exchange(msg), khi, klo, thi, tlo, q1, stats,
    )
    msg, stats = call(
        functools.partial(model_kernel, 4, True),
        [((AF * LAST, 128), F32), stat],
        exchange(msg), cut, tables, stats, s1, s2,
    )
    arrived = exchange(msg)
    [stats] = call(stats_kernel, [stat], arrived, stats)
    [pair] = call(pair_kernel, [((16, 128), F32)], stats, lax.ppermute(stats, "vert", [(i, i ^ 1) for i in range(VERT)]))
    gathered = [pair] + [lax.ppermute(pair, "vert", [(i, i ^ (2 * d)) for i in range(VERT)]) for d in (1, 2, 3)]
    out = ((VB, TB, RECV), F32)
    return tuple(
        call(
            last_kernel,
            [out, out, data],
            arrived, *gathered, recorded, q1, q2,
            scratch=[pltpu.VMEM((64, 128), F32)],
        )
    )


def solution(mesh):
    in_specs = (P("af", "vert", None), P("af", None, None, None), P())
    out_specs = (P("vert", "af", None), P("vert", "af", None), P("af", "vert", None))
    return jax.shard_map(
        per_device, mesh=mesh, in_specs=in_specs, out_specs=out_specs, check_vma=False
    )
```

```python
import functools
import math

import jax
import jax.numpy as jnp
import numpy as np
from jax import lax
from jax.experimental import pallas as pl
from jax.experimental.pallas import tpu as pltpu
from jax.sharding import PartitionSpec as P

FREQS = 256
SAMPLES = 512
RECV = 512
SRCS = 96
EPSILON = 1e-06
F32 = jnp.float32
BF16 = jnp.bfloat16

AF = 32
VERT = 8
FB = FREQS // AF
VB = 8
QB = RECV // 128
KB = 2 * FB
MSG = KB + 1
TB = SAMPLES // AF
LAST = 3 * TB + 1
CHUNKS = ((0, 2), (2, 2), (4, 2), (6, 2))


def dft_tables():
    times = np.arange(SAMPLES)
    freqs = np.arange(FREQS)
    angles = 2.0 * math.pi / SAMPLES * ((times[:, None] * freqs[None, :]) % SAMPLES)
    scale = 1.0 / math.sqrt(SAMPLES)
    table = np.stack([np.cos(angles), -np.sin(angles)], axis=2) * scale
    table = table.reshape(SAMPLES, 2 * FREQS).astype(np.float32)
    out = []
    for t in (table, np.ascontiguousarray(table.T)):
        hi = t.astype(jnp.bfloat16)
        out += [hi, (t - hi.astype(np.float32)).astype(jnp.bfloat16)]
    return np.stack(out)


def split(x):
    hi = x.astype(BF16)
    return hi, (x - hi.astype(F32)).astype(BF16)


def dot(a, b):
    return lax.dot_general(a, b, (((1,), (0,)), ((), ())), preferred_element_type=F32)


def dot_nt(a, b):
    return lax.dot_general(a, b, (((1,), (1,)), ((), ())), preferred_element_type=F32)


def turned(x, sign):
    return jnp.concatenate([sign * x[:, SRCS:], -sign * x[:, :SRCS]], axis=1)


def kernel_adjoint(u, khi, klo):
    hi, lo = split(jnp.concatenate([u, turned(u, 1.0)], axis=0))
    both = dot(jnp.concatenate([hi, lo], axis=0), khi)
    return both[: 2 * VB] + both[2 * VB :] + dot(hi, klo)


def kernel_forward(x, khi, klo, product):
    hi, lo = split(x)
    both = product(jnp.concatenate([hi, lo], axis=0), khi)
    y = both[: 2 * VB] + both[2 * VB :] + product(hi, klo)
    return y[:VB] + turned(y[VB:], -1.0)


def on_core(core):
    return lax.rem(lax.axis_index("vert"), 2) == core


def ratio(a, b):
    return jnp.where(b > 0, a / jnp.where(b > 0, b, 1.0), 0.0)


def arrived_sum(recv, pitch):
    rows = recv[pl.ds(pitch - 1, AF, stride=pitch), :]
    return jnp.broadcast_to(jnp.sum(rows, keepdims=True), (1, 128))


def lane_zero(total):
    lane = lax.broadcasted_iota(jnp.int32, (1, 128), 1)
    return jnp.where(lane == 0, jnp.broadcast_to(total, (1, 128)), 0.0)


def put_spectra(msg, f, z, pitch):
    for c in range(2):
        for q in range(QB):
            msg[pl.ds(q * pitch + 2 * f + c, VB, stride=QB * pitch), :] = z[
                c * VB : (c + 1) * VB, q * 128 : (q + 1) * 128
            ]


def put_partial(msg, row, pitch):
    for d in range(AF):
        msg[pl.ds(d * pitch + pitch - 1, 1), :] = row


def halves_kernel(k_hbm, khi_ref, klo_ref, k_buf, sems):
    copies = [
        pltpu.make_async_copy(k_hbm.at[pl.ds(at, n)], k_buf.at[pl.ds(at, n)], sems.at[i])
        for i, (at, n) in enumerate(CHUNKS)
    ]
    for copy in copies:
        copy.start()
    for copy, (at, n) in zip(copies, CHUNKS):
        copy.wait()
        for f in range(at, at + n):
            khi_ref[f], klo_ref[f] = split(k_buf[f])


def first_kernel(u_ref, khi_ref, klo_ref, msg, square_ref, thi_ref, tlo_ref):
    square = jnp.zeros((VB, 2 * SRCS), F32)
    for f in range(FB):
        u = u_ref[f]
        square += u * u
        put_spectra(msg, f, kernel_adjoint(u, khi_ref[f], klo_ref[f]), KB)
    square_ref[...] = jnp.broadcast_to(jnp.sum(square, keepdims=True), (1, 128))

    @pl.when(on_core(0))
    def _():
        for f in range(FB):
            thi_ref[f] = khi_ref[f].T
            tlo_ref[f] = klo_ref[f].T


def data_kernel(
    order, recv, khi_ref, klo_ref, thi_ref, tlo_ref, before_ref, stats, msg, q_ref, stats_out
):
    if order == 1:
        rows = jnp.sum(recv[pl.ds(KB, AF, stride=MSG), :], axis=0, keepdims=True)
        low = lax.broadcasted_iota(jnp.int32, (1, 128), 1) < 64
        total, first = [
            jnp.broadcast_to(jnp.sum(jnp.where(half, rows, 0.0), keepdims=True), (1, 128))
            for half in (low, ~low)
        ]
        stats_out[...] = jnp.zeros((8, 128), F32)
        stats_out[pl.ds(0, 1), :] = first
    else:
        total = arrived_sum(recv, MSG)
        first = stats[pl.ds(order - 1, 1), :]
        stats_out[...] = stats[...]
    stats_out[pl.ds(order, 1), :] = total
    coefficient = ratio(total, first)[:, :1]

    def step(hi_ref, lo_ref, product):
        square = jnp.zeros((VB, 2 * SRCS), F32)
        steps = []
        for f in range(FB):
            x = jnp.concatenate(
                [
                    jnp.concatenate(
                        [
                            recv[pl.ds(q * MSG + 2 * f + c, VB, stride=QB * MSG), :]
                            for q in range(QB)
                        ],
                        axis=1,
                    )
                    for c in range(2)
                ],
                axis=0,
            )
            u = kernel_forward(x, hi_ref[f], lo_ref[f], product) - coefficient * before_ref[f]
            q_ref[f] = u
            square += u * u
            steps.append(u)
        for f in range(FB):
            put_spectra(msg, f, kernel_adjoint(steps[f], khi_ref[f], klo_ref[f]), MSG)
        put_partial(msg, lane_zero(jnp.sum(square, keepdims=True)), MSG)

    pl.when(on_core(0))(lambda: step(thi_ref, tlo_ref, dot))
    pl.when(on_core(1))(lambda: step(khi_ref, klo_ref, dot_nt))


def table_apply(table_ref, at, x):
    hi, lo = split(x)
    both = dot(table_ref[at], jnp.concatenate([hi, lo], axis=1))
    return both[:, :128] + both[:, 128:] + dot(table_ref[at + 1], hi)


def model_kernel(order, last, *refs):
    refs = list(refs)
    recv, cut_ref, table_ref = refs[:3]
    refs = refs[3:]
    stats = refs.pop(0)
    if order > 0:
        earlier = [refs.pop(0) for _ in range(order // 2)]
        total = arrived_sum(recv, MSG)
        spectra = jnp.concatenate([recv[pl.ds(p * MSG, KB), :] for p in range(AF)], axis=0)
    else:
        spectra = recv[...]
    s = table_apply(table_ref, 0, spectra)
    if order > 0:
        s = s - ratio(total, stats[pl.ds(order - 1, 1), :]) * earlier[-1][...]
    cut = cut_ref[pl.ds(lax.rem(lax.axis_index("af"), QB), 1), :]
    keep = lax.broadcasted_iota(jnp.int32, (SAMPLES, 128), 0) < cut
    s = jnp.where(keep, s, 0.0)
    partial = jnp.sum(s * s, axis=0, keepdims=True)
    if order == 0:
        lane = lax.broadcasted_iota(jnp.int32, (1, 128), 1)
        whole = jnp.broadcast_to(jnp.sum(partial, keepdims=True), (1, 128))
        partial = jnp.where(lane == 0, whole, jnp.where(lane == 64, stats[...], 0.0))
    msg = refs.pop(0)
    if not last:
        s_ref = refs.pop(0)
        s_ref[...] = s
    if order > 0:
        [stats_out] = refs
        stats_out[...] = stats[...]
        stats_out[pl.ds(order, 1), :] = total
    if last:
        for j, value in enumerate([e[...] for e in earlier] + [s]):
            for p in range(AF):
                msg[pl.ds(p * LAST + j * TB, TB), :] = value[p * TB : (p + 1) * TB]
        put_partial(msg, partial, LAST)
    else:
        out = table_apply(table_ref, 2, s)
        for p in range(AF):
            msg[pl.ds(p * MSG, KB), :] = out[p * KB : (p + 1) * KB]
        put_partial(msg, partial, MSG)


def stats_kernel(recv, stats, out):
    total = arrived_sum(recv, LAST)
    row = lax.broadcasted_iota(jnp.int32, (8, 128), 0)
    out[...] = jnp.where(row == 5, total, stats[...])


def pair_kernel(mine, other, out):
    out[pl.ds(0, 8), :] = mine[...]
    out[pl.ds(8, 8), :] = other[...]


def last_kernel(recv, g0, g1, g2, g3, q0_ref, q1_ref, q2_ref, sol_ref, dir_ref, left_ref, rows):
    gathered = (g0, g1, g2, g3)
    n0, m1, n1, m2, n2, m3 = [
        jnp.concatenate([g[pl.ds(8 * c + j, 1), :] for g in gathered for c in range(2)], axis=0)
        for j in range(6)
    ]

    def norm(x):
        return jnp.sqrt(jnp.sum(x, axis=0, keepdims=True) + EPSILON)

    theta, kappa, lam, mu = ratio(m1, n0), ratio(n1, m1), ratio(m2, n1), ratio(n2, m2)
    beta0 = norm(n0)
    alpha1 = norm(m1 / (beta0 * beta0))
    e = 1.0 / (beta0 * alpha1)
    d = e * theta - alpha1 / beta0
    beta1 = norm(e * e * n1 + d * d * n0)
    f1 = e / beta1
    f0 = d / beta1
    h = f1 * kappa + f0 - beta1 * e
    alpha2 = norm(f1 * f1 * m2 + h * h * m1)
    g2 = f1 / alpha2
    g1 = h / alpha2
    rho1 = jnp.sqrt(alpha1 * alpha1 + beta1 * beta1)
    cos1, sin1 = alpha1 / rho1, beta1 / rho1
    theta1 = sin1 * alpha2
    rhobar = -cos1 * alpha2
    phi1, phibar = cos1 * beta0, sin1 * beta0
    w2 = g2
    w1 = g1 - theta1 / rho1 * e
    c2 = g2
    c1 = g2 * lam + g1 - alpha2 * f1
    c0 = g1 * theta - alpha2 * f0
    beta2 = norm(c2 * c2 * n2 + c1 * c1 * n1 + c0 * c0 * n0)
    c2, c1, c0 = c2 / beta2, c1 / beta2, c0 / beta2
    z3 = c2
    z2 = c2 * mu + c1 - beta2 * g2
    z1 = c1 * kappa + c0 - beta2 * g1
    alpha3 = norm(z3 * z3 * m3 + z2 * z2 * m2 + z1 * z1 * m1)
    rho2 = jnp.sqrt(rhobar * rhobar + beta2 * beta2)
    cos2, sin2 = rhobar / rho2, beta2 / rho2
    step2 = cos2 * phibar / rho2
    turn2 = sin2 * alpha3 / rho2
    x1 = phi1 / rho1 * e + step2 * w1
    x2 = step2 * w2
    y1 = z1 / alpha3 - turn2 * w1
    y2 = z2 / alpha3 - turn2 * w2
    y3 = z3 / alpha3
    for j, value in enumerate((x1, x2, y1, y2, y3, c0, c1, c2)):
        rows[pl.ds(8 * j, 8), :] = jnp.broadcast_to(value, (VERT, 128))
    group = 0
    x1, x2, y1, y2, y3, c0, c1, c2 = [rows[pl.ds(8 * j + group, 1), :] for j in range(8)]
    for v in range(VB):
        for q in range(QB):
            at = (v * QB + q) * LAST
            s1, s2, s3 = [recv[pl.ds(at + j * TB, TB), :] for j in range(3)]
            sol_ref[v, :, q * 128 : (q + 1) * 128] = x1 * s1 + x2 * s2
            dir_ref[v, :, q * 128 : (q + 1) * 128] = y1 * s1 + y2 * s2 + y3 * s3
    c0, c1, c2 = c0[:, :1], c1[:, :1], c2[:, :1]
    for f in range(FB):
        left_ref[f] = c0 * q0_ref[f] + c1 * q1_ref[f] + c2 * q2_ref[f]


def call(body, outs, *operands, scratch=(), space=pltpu.VMEM, vmem=16):
    here = pl.BlockSpec(memory_space=pltpu.VMEM)
    return pl.pallas_call(
        body,
        out_shape=[jax.ShapeDtypeStruct(s, t) for s, t in outs],
        in_specs=[pl.BlockSpec(memory_space=space)] * len(operands),
        out_specs=[here] * len(outs),
        scratch_shapes=list(scratch),
        compiler_params=pltpu.CompilerParams(vmem_limit_bytes=vmem * 1024 * 1024),
    )(*operands)


def exchange(message):
    flat = message.reshape(AF, 1, message.shape[0] // AF * 128)
    flat = lax.all_to_all(flat, "af", split_axis=0, concat_axis=0, tiled=True)
    return flat.reshape(message.shape)


def per_device(recorded, kernel, cutoff):
    tables = jnp.asarray(dft_tables())
    cut = cutoff.reshape(QB, 128)
    kernel = kernel.reshape(FB, 2 * SRCS, RECV)
    message = ((AF * MSG, 128), F32)
    data = ((FB, VB, 2 * SRCS), F32)
    model = ((SAMPLES, 128), F32)
    stat = ((8, 128), F32)
    wide = ((FB, 2 * SRCS, RECV), BF16)

    khi, klo = call(
        halves_kernel,
        [wide, wide],
        kernel,
        scratch=[pltpu.VMEM(kernel.shape, F32), pltpu.SemaphoreType.DMA((len(CHUNKS),))],
        space=pltpu.HBM,
        vmem=49,
    )
    turned_halves = ((FB, RECV, 2 * SRCS), BF16)
    msg, square, thi, tlo = call(
        first_kernel,
        [((AF * KB, 128), F32), ((1, 128), F32), turned_halves, turned_halves],
        recorded, khi, klo,
    )
    msg, s1 = call(
        functools.partial(model_kernel, 0, False),
        [message, model],
        exchange(msg), cut, tables, square,
    )
    msg, q1, stats = call(
        functools.partial(data_kernel, 1),
        [message, data, stat],
        exchange(msg), khi, klo, thi, tlo, recorded, square,
    )
    msg, s2, stats = call(
        functools.partial(model_kernel, 2, False),
        [message, model, stat],
        exchange(msg), cut, tables, stats, s1,
    )
    msg, q2, stats = call(
        functools.partial(data_kernel, 3),
        [message, data, stat],
        exchange(msg), khi, klo, thi, tlo, q1, stats,
    )
    msg, stats = call(
        functools.partial(model_kernel, 4, True),
        [((AF * LAST, 128), F32), stat],
        exchange(msg), cut, tables, stats, s1, s2,
    )
    arrived = exchange(msg)
    [stats] = call(stats_kernel, [stat], arrived, stats)
    [pair] = call(pair_kernel, [((16, 128), F32)], stats, lax.ppermute(stats, "vert", [(i, i ^ 1) for i in range(VERT)]))
    gathered = [pair] + [lax.ppermute(pair, "vert", [(i, i ^ (2 * d)) for i in range(VERT)]) for d in (1, 2, 3)]
    out = ((VB, TB, RECV), F32)
    return tuple(
        call(
            last_kernel,
            [out, out, data],
            arrived, *gathered, recorded, q1, q2,
            scratch=[pltpu.VMEM((64, 128), F32)],
        )
    )


def solution(mesh):
    in_specs = (P("af", "vert", None), P("af", None, None, None), P())
    out_specs = (P("vert", "af", None), P("vert", "af", None), P("af", "vert", None))
    return jax.shard_map(
        per_device, mesh=mesh, in_specs=in_specs, out_specs=out_specs, check_vma=False
    )
```

```python
import functools
import math

import jax
import jax.numpy as jnp
import numpy as np
from jax import lax
from jax.experimental import pallas as pl
from jax.experimental.pallas import tpu as pltpu
from jax.sharding import PartitionSpec as P

FREQS = 256
SAMPLES = 512
RECV = 512
SRCS = 96
EPSILON = 1e-06
F32 = jnp.float32
BF16 = jnp.bfloat16

AF = 32
VERT = 8
FB = FREQS // AF
VB = 8
QB = RECV // 128
KB = 2 * FB
MSG = KB + 1
TB = SAMPLES // AF
LAST = 3 * TB + 1
CHUNKS = tuple((f, 1) for f in range(FB))


def dft_tables():
    times = np.arange(SAMPLES)
    freqs = np.arange(FREQS)
    angles = 2.0 * math.pi / SAMPLES * ((times[:, None] * freqs[None, :]) % SAMPLES)
    scale = 1.0 / math.sqrt(SAMPLES)
    table = np.stack([np.cos(angles), -np.sin(angles)], axis=2) * scale
    table = table.reshape(SAMPLES, 2 * FREQS).astype(np.float32)
    out = []
    for t in (table, np.ascontiguousarray(table.T)):
        hi = t.astype(jnp.bfloat16)
        out += [hi, (t - hi.astype(np.float32)).astype(jnp.bfloat16)]
    return np.stack(out)


def split(x):
    hi = x.astype(BF16)
    return hi, (x - hi.astype(F32)).astype(BF16)


def dot(a, b):
    return lax.dot_general(a, b, (((1,), (0,)), ((), ())), preferred_element_type=F32)


def dot_nt(a, b):
    return lax.dot_general(a, b, (((1,), (1,)), ((), ())), preferred_element_type=F32)


def turned(x, sign):
    return jnp.concatenate([sign * x[:, SRCS:], -sign * x[:, :SRCS]], axis=1)


def kernel_adjoint(u, khi, klo):
    hi, lo = split(jnp.concatenate([u, turned(u, 1.0)], axis=0))
    both = dot(jnp.concatenate([hi, lo], axis=0), khi)
    return both[: 2 * VB] + both[2 * VB :] + dot(hi, klo)


def kernel_forward(x, khi, klo, product):
    hi, lo = split(x)
    both = product(jnp.concatenate([hi, lo], axis=0), khi)
    y = both[: 2 * VB] + both[2 * VB :] + product(hi, klo)
    return y[:VB] + turned(y[VB:], -1.0)


def on_core(core):
    return lax.rem(lax.axis_index("vert"), 2) == core


def ratio(a, b):
    return jnp.where(b > 0, a / jnp.where(b > 0, b, 1.0), 0.0)


def arrived_sum(recv, pitch):
    rows = recv[pl.ds(pitch - 1, AF, stride=pitch), :]
    return jnp.broadcast_to(jnp.sum(rows, keepdims=True), (1, 128))


def lane_zero(total):
    lane = lax.broadcasted_iota(jnp.int32, (1, 128), 1)
    return jnp.where(lane == 0, jnp.broadcast_to(total, (1, 128)), 0.0)


def put_spectra(msg, f, z, pitch):
    for c in range(2):
        for q in range(QB):
            msg[pl.ds(q * pitch + 2 * f + c, VB, stride=QB * pitch), :] = z[
                c * VB : (c + 1) * VB, q * 128 : (q + 1) * 128
            ]


def put_partial(msg, row, pitch):
    for d in range(AF):
        msg[pl.ds(d * pitch + pitch - 1, 1), :] = row


def halves_kernel(k_hbm, khi_ref, klo_ref, k_buf, sems):
    copies = [
        pltpu.make_async_copy(k_hbm.at[pl.ds(at, n)], k_buf.at[pl.ds(at, n)], sems.at[i])
        for i, (at, n) in enumerate(CHUNKS)
    ]
    for copy in copies:
        copy.start()
    for copy, (at, n) in zip(copies, CHUNKS):
        copy.wait()
        for f in range(at, at + n):
            khi_ref[f], klo_ref[f] = split(k_buf[f])


def first_kernel(u_ref, khi_ref, klo_ref, msg, square_ref, thi_ref, tlo_ref):
    square = jnp.zeros((VB, 2 * SRCS), F32)
    for f in range(FB):
        u = u_ref[f]
        square += u * u
        put_spectra(msg, f, kernel_adjoint(u, khi_ref[f], klo_ref[f]), KB)
    square_ref[...] = jnp.broadcast_to(jnp.sum(square, keepdims=True), (1, 128))

    @pl.when(on_core(0))
    def _():
        for f in range(FB):
            thi_ref[f] = khi_ref[f].T
            tlo_ref[f] = klo_ref[f].T


def data_kernel(
    order, recv, khi_ref, klo_ref, thi_ref, tlo_ref, before_ref, stats, msg, q_ref, stats_out
):
    if order == 1:
        rows = jnp.sum(recv[pl.ds(KB, AF, stride=MSG), :], axis=0, keepdims=True)
        low = lax.broadcasted_iota(jnp.int32, (1, 128), 1) < 64
        total, first = [
            jnp.broadcast_to(jnp.sum(jnp.where(half, rows, 0.0), keepdims=True), (1, 128))
            for half in (low, ~low)
        ]
        stats_out[...] = jnp.zeros((8, 128), F32)
        stats_out[pl.ds(0, 1), :] = first
    else:
        total = arrived_sum(recv, MSG)
        first = stats[pl.ds(order - 1, 1), :]
        stats_out[...] = stats[...]
    stats_out[pl.ds(order, 1), :] = total
    coefficient = ratio(total, first)[:, :1]

    def step(hi_ref, lo_ref, product):
        square = jnp.zeros((VB, 2 * SRCS), F32)
        steps = []
        for f in range(FB):
            x = jnp.concatenate(
                [
                    jnp.concatenate(
                        [
                            recv[pl.ds(q * MSG + 2 * f + c, VB, stride=QB * MSG), :]
                            for q in range(QB)
                        ],
                        axis=1,
                    )
                    for c in range(2)
                ],
                axis=0,
            )
            u = kernel_forward(x, hi_ref[f], lo_ref[f], product) - coefficient * before_ref[f]
            q_ref[f] = u
            square += u * u
            steps.append(u)
        for f in range(FB):
            put_spectra(msg, f, kernel_adjoint(steps[f], khi_ref[f], klo_ref[f]), MSG)
        put_partial(msg, lane_zero(jnp.sum(square, keepdims=True)), MSG)

    pl.when(on_core(0))(lambda: step(thi_ref, tlo_ref, dot))
    pl.when(on_core(1))(lambda: step(khi_ref, klo_ref, dot_nt))


def table_apply(table_ref, at, x):
    hi, lo = split(x)
    both = dot(table_ref[at], jnp.concatenate([hi, lo], axis=1))
    return both[:, :128] + both[:, 128:] + dot(table_ref[at + 1], hi)


def model_kernel(order, last, *refs):
    refs = list(refs)
    recv, cut_ref, table_ref = refs[:3]
    refs = refs[3:]
    stats = refs.pop(0)
    if order > 0:
        earlier = [refs.pop(0) for _ in range(order // 2)]
        total = arrived_sum(recv, MSG)
        spectra = jnp.concatenate([recv[pl.ds(p * MSG, KB), :] for p in range(AF)], axis=0)
    else:
        spectra = recv[...]
    s = table_apply(table_ref, 0, spectra)
    if order > 0:
        s = s - ratio(total, stats[pl.ds(order - 1, 1), :]) * earlier[-1][...]
    cut = cut_ref[pl.ds(lax.rem(lax.axis_index("af"), QB), 1), :]
    keep = lax.broadcasted_iota(jnp.int32, (SAMPLES, 128), 0) < cut
    s = jnp.where(keep, s, 0.0)
    partial = jnp.sum(s * s, axis=0, keepdims=True)
    if order == 0:
        lane = lax.broadcasted_iota(jnp.int32, (1, 128), 1)
        whole = jnp.broadcast_to(jnp.sum(partial, keepdims=True), (1, 128))
        partial = jnp.where(lane == 0, whole, jnp.where(lane == 64, stats[...], 0.0))
    msg = refs.pop(0)
    if not last:
        s_ref = refs.pop(0)
        s_ref[...] = s
    if order > 0:
        [stats_out] = refs
        stats_out[...] = stats[...]
        stats_out[pl.ds(order, 1), :] = total
    if last:
        for j, value in enumerate([e[...] for e in earlier] + [s]):
            for p in range(AF):
                msg[pl.ds(p * LAST + j * TB, TB), :] = value[p * TB : (p + 1) * TB]
        put_partial(msg, partial, LAST)
    else:
        out = table_apply(table_ref, 2, s)
        for p in range(AF):
            msg[pl.ds(p * MSG, KB), :] = out[p * KB : (p + 1) * KB]
        put_partial(msg, partial, MSG)


def stats_kernel(recv, stats, out):
    total = arrived_sum(recv, LAST)
    row = lax.broadcasted_iota(jnp.int32, (8, 128), 0)
    out[...] = jnp.where(row == 5, total, stats[...])


def pair_kernel(mine, other, out):
    out[pl.ds(0, 8), :] = mine[...]
    out[pl.ds(8, 8), :] = other[...]


def last_kernel(recv, g0, g1, g2, g3, q0_ref, q1_ref, q2_ref, sol_ref, dir_ref, left_ref, rows):
    gathered = (g0, g1, g2, g3)
    n0, m1, n1, m2, n2, m3 = [
        jnp.concatenate([g[pl.ds(8 * c + j, 1), :] for g in gathered for c in range(2)], axis=0)
        for j in range(6)
    ]

    def norm(x):
        return jnp.sqrt(jnp.sum(x, axis=0, keepdims=True) + EPSILON)

    theta, kappa, lam, mu = ratio(m1, n0), ratio(n1, m1), ratio(m2, n1), ratio(n2, m2)
    beta0 = norm(n0)
    alpha1 = norm(m1 / (beta0 * beta0))
    e = 1.0 / (beta0 * alpha1)
    d = e * theta - alpha1 / beta0
    beta1 = norm(e * e * n1 + d * d * n0)
    f1 = e / beta1
    f0 = d / beta1
    h = f1 * kappa + f0 - beta1 * e
    alpha2 = norm(f1 * f1 * m2 + h * h * m1)
    g2 = f1 / alpha2
    g1 = h / alpha2
    rho1 = jnp.sqrt(alpha1 * alpha1 + beta1 * beta1)
    cos1, sin1 = alpha1 / rho1, beta1 / rho1
    theta1 = sin1 * alpha2
    rhobar = -cos1 * alpha2
    phi1, phibar = cos1 * beta0, sin1 * beta0
    w2 = g2
    w1 = g1 - theta1 / rho1 * e
    c2 = g2
    c1 = g2 * lam + g1 - alpha2 * f1
    c0 = g1 * theta - alpha2 * f0
    beta2 = norm(c2 * c2 * n2 + c1 * c1 * n1 + c0 * c0 * n0)
    c2, c1, c0 = c2 / beta2, c1 / beta2, c0 / beta2
    z3 = c2
    z2 = c2 * mu + c1 - beta2 * g2
    z1 = c1 * kappa + c0 - beta2 * g1
    alpha3 = norm(z3 * z3 * m3 + z2 * z2 * m2 + z1 * z1 * m1)
    rho2 = jnp.sqrt(rhobar * rhobar + beta2 * beta2)
    cos2, sin2 = rhobar / rho2, beta2 / rho2
    step2 = cos2 * phibar / rho2
    turn2 = sin2 * alpha3 / rho2
    x1 = phi1 / rho1 * e + step2 * w1
    x2 = step2 * w2
    y1 = z1 / alpha3 - turn2 * w1
    y2 = z2 / alpha3 - turn2 * w2
    y3 = z3 / alpha3
    for j, value in enumerate((x1, x2, y1, y2, y3, c0, c1, c2)):
        rows[pl.ds(8 * j, 8), :] = jnp.broadcast_to(value, (VERT, 128))
    group = 0
    x1, x2, y1, y2, y3, c0, c1, c2 = [rows[pl.ds(8 * j + group, 1), :] for j in range(8)]
    for v in range(VB):
        for q in range(QB):
            at = (v * QB + q) * LAST
            s1, s2, s3 = [recv[pl.ds(at + j * TB, TB), :] for j in range(3)]
            sol_ref[v, :, q * 128 : (q + 1) * 128] = x1 * s1 + x2 * s2
            dir_ref[v, :, q * 128 : (q + 1) * 128] = y1 * s1 + y2 * s2 + y3 * s3
    c0, c1, c2 = c0[:, :1], c1[:, :1], c2[:, :1]
    for f in range(FB):
        left_ref[f] = c0 * q0_ref[f] + c1 * q1_ref[f] + c2 * q2_ref[f]


def call(body, outs, *operands, scratch=(), space=pltpu.VMEM, vmem=16):
    here = pl.BlockSpec(memory_space=pltpu.VMEM)
    return pl.pallas_call(
        body,
        out_shape=[jax.ShapeDtypeStruct(s, t) for s, t in outs],
        in_specs=[pl.BlockSpec(memory_space=space)] * len(operands),
        out_specs=[here] * len(outs),
        scratch_shapes=list(scratch),
        compiler_params=pltpu.CompilerParams(vmem_limit_bytes=vmem * 1024 * 1024),
    )(*operands)


def exchange(message):
    flat = message.reshape(AF, 1, message.shape[0] // AF * 128)
    flat = lax.all_to_all(flat, "af", split_axis=0, concat_axis=0, tiled=True)
    return flat.reshape(message.shape)


def per_device(recorded, kernel, cutoff):
    tables = jnp.asarray(dft_tables())
    cut = cutoff.reshape(QB, 128)
    kernel = kernel.reshape(FB, 2 * SRCS, RECV)
    message = ((AF * MSG, 128), F32)
    data = ((FB, VB, 2 * SRCS), F32)
    model = ((SAMPLES, 128), F32)
    stat = ((8, 128), F32)
    wide = ((FB, 2 * SRCS, RECV), BF16)

    khi, klo = call(
        halves_kernel,
        [wide, wide],
        kernel,
        scratch=[pltpu.VMEM(kernel.shape, F32), pltpu.SemaphoreType.DMA((len(CHUNKS),))],
        space=pltpu.HBM,
        vmem=49,
    )
    turned_halves = ((FB, RECV, 2 * SRCS), BF16)
    msg, square, thi, tlo = call(
        first_kernel,
        [((AF * KB, 128), F32), ((1, 128), F32), turned_halves, turned_halves],
        recorded, khi, klo,
    )
    msg, s1 = call(
        functools.partial(model_kernel, 0, False),
        [message, model],
        exchange(msg), cut, tables, square,
    )
    msg, q1, stats = call(
        functools.partial(data_kernel, 1),
        [message, data, stat],
        exchange(msg), khi, klo, thi, tlo, recorded, square,
    )
    msg, s2, stats = call(
        functools.partial(model_kernel, 2, False),
        [message, model, stat],
        exchange(msg), cut, tables, stats, s1,
    )
    msg, q2, stats = call(
        functools.partial(data_kernel, 3),
        [message, data, stat],
        exchange(msg), khi, klo, thi, tlo, q1, stats,
    )
    msg, stats = call(
        functools.partial(model_kernel, 4, True),
        [((AF * LAST, 128), F32), stat],
        exchange(msg), cut, tables, stats, s1, s2,
    )
    arrived = exchange(msg)
    [stats] = call(stats_kernel, [stat], arrived, stats)
    [pair] = call(pair_kernel, [((16, 128), F32)], stats, lax.ppermute(stats, "vert", [(i, i ^ 1) for i in range(VERT)]))
    gathered = [pair] + [lax.ppermute(pair, "vert", [(i, i ^ (2 * d)) for i in range(VERT)]) for d in (1, 2, 3)]
    out = ((VB, TB, RECV), F32)
    return tuple(
        call(
            last_kernel,
            [out, out, data],
            arrived, *gathered, recorded, q1, q2,
            scratch=[pltpu.VMEM((64, 128), F32)],
        )
    )


def solution(mesh):
    in_specs = (P("af", "vert", None), P("af", None, None, None), P())
    out_specs = (P("vert", "af", None), P("vert", "af", None), P("af", "vert", None))
    return jax.shard_map(
        per_device, mesh=mesh, in_specs=in_specs, out_specs=out_specs, check_vma=False
    )
```

```python
import functools
import math

import jax
import jax.numpy as jnp
import numpy as np
from jax import lax
from jax.experimental import pallas as pl
from jax.experimental.pallas import tpu as pltpu
from jax.sharding import PartitionSpec as P

FREQS = 256
SAMPLES = 512
RECV = 512
SRCS = 96
EPSILON = 1e-06
F32 = jnp.float32
BF16 = jnp.bfloat16

AF = 32
VERT = 8
FB = FREQS // AF
VB = 8
QB = RECV // 128
KB = 2 * FB
MSG = KB + 1
TB = SAMPLES // AF
LAST = 3 * TB + 1
CHUNKS = tuple((f, 1) for f in range(FB))


def dft_tables():
    times = np.arange(SAMPLES)
    freqs = np.arange(FREQS)
    angles = 2.0 * math.pi / SAMPLES * ((times[:, None] * freqs[None, :]) % SAMPLES)
    scale = 1.0 / math.sqrt(SAMPLES)
    table = np.stack([np.cos(angles), -np.sin(angles)], axis=2) * scale
    table = table.reshape(SAMPLES, 2 * FREQS).astype(np.float32)
    out = []
    for t in (table, np.ascontiguousarray(table.T)):
        hi = t.astype(jnp.bfloat16)
        out += [hi, (t - hi.astype(np.float32)).astype(jnp.bfloat16)]
    return np.stack(out)


def split(x):
    hi = x.astype(BF16)
    return hi, (x - hi.astype(F32)).astype(BF16)


def dot(a, b):
    return lax.dot_general(a, b, (((1,), (0,)), ((), ())), preferred_element_type=F32)


def dot_nt(a, b):
    return lax.dot_general(a, b, (((1,), (1,)), ((), ())), preferred_element_type=F32)


def turned(x, sign):
    return jnp.concatenate([sign * x[:, SRCS:], -sign * x[:, :SRCS]], axis=1)


def kernel_adjoint(u, khi, klo):
    hi, lo = split(jnp.concatenate([u, turned(u, 1.0)], axis=0))
    both = dot(jnp.concatenate([hi, lo], axis=0), khi)
    return both[: 2 * VB] + both[2 * VB :] + dot(hi, klo)


def kernel_forward(x, khi, klo, product):
    hi, lo = split(x)
    both = product(jnp.concatenate([hi, lo], axis=0), khi)
    y = both[: 2 * VB] + both[2 * VB :] + product(hi, klo)
    return y[:VB] + turned(y[VB:], -1.0)


def on_core(core):
    return lax.rem(lax.axis_index("vert"), 2) == core


def ratio(a, b):
    return jnp.where(b > 0, a / jnp.where(b > 0, b, 1.0), 0.0)


def arrived_sum(recv, pitch):
    rows = recv[pl.ds(pitch - 1, AF, stride=pitch), :]
    return jnp.broadcast_to(jnp.sum(rows, keepdims=True), (1, 128))


def lane_zero(total):
    lane = lax.broadcasted_iota(jnp.int32, (1, 128), 1)
    return jnp.where(lane == 0, jnp.broadcast_to(total, (1, 128)), 0.0)


def put_spectra(msg, f, z, pitch):
    for c in range(2):
        for q in range(QB):
            msg[pl.ds(q * pitch + 2 * f + c, VB, stride=QB * pitch), :] = z[
                c * VB : (c + 1) * VB, q * 128 : (q + 1) * 128
            ]


def put_partial(msg, row, pitch):
    for d in range(AF):
        msg[pl.ds(d * pitch + pitch - 1, 1), :] = row


def halves_kernel(k_hbm, khi_ref, klo_ref, k_buf, sems):
    copies = [
        pltpu.make_async_copy(k_hbm.at[pl.ds(at, n)], k_buf.at[pl.ds(at, n)], sems.at[i])
        for i, (at, n) in enumerate(CHUNKS)
    ]
    for copy in copies:
        copy.start()
    for copy, (at, n) in zip(copies, CHUNKS):
        copy.wait()
        for f in range(at, at + n):
            khi_ref[f], klo_ref[f] = split(k_buf[f])


def first_kernel(u_ref, khi_ref, klo_ref, msg, square_ref, thi_ref, tlo_ref):
    square = jnp.zeros((VB, 2 * SRCS), F32)
    for f in range(FB):
        u = u_ref[f]
        square += u * u
        put_spectra(msg, f, kernel_adjoint(u, khi_ref[f], klo_ref[f]), KB)
    square_ref[...] = jnp.broadcast_to(jnp.sum(square, keepdims=True), (1, 128))

    @pl.when(on_core(0))
    def _():
        for f in range(FB):
            thi_ref[f] = khi_ref[f].T
            tlo_ref[f] = klo_ref[f].T


def data_kernel(
    order, recv, khi_ref, klo_ref, thi_ref, tlo_ref, before_ref, stats, msg, q_ref, stats_out
):
    if order == 1:
        rows = jnp.sum(recv[pl.ds(KB, AF, stride=MSG), :], axis=0, keepdims=True)
        low = lax.broadcasted_iota(jnp.int32, (1, 128), 1) < 64
        total, first = [
            jnp.broadcast_to(jnp.sum(jnp.where(half, rows, 0.0), keepdims=True), (1, 128))
            for half in (low, ~low)
        ]
        stats_out[...] = jnp.zeros((8, 128), F32)
        stats_out[pl.ds(0, 1), :] = first
    else:
        total = arrived_sum(recv, MSG)
        first = stats[pl.ds(order - 1, 1), :]
        stats_out[...] = stats[...]
    stats_out[pl.ds(order, 1), :] = total
    coefficient = ratio(total, first)[:, :1]

    def step(hi_ref, lo_ref, product):
        square = jnp.zeros((VB, 2 * SRCS), F32)
        steps = []
        for f in range(FB):
            x = jnp.concatenate(
                [
                    jnp.concatenate(
                        [
                            recv[pl.ds(q * MSG + 2 * f + c, VB, stride=QB * MSG), :]
                            for q in range(QB)
                        ],
                        axis=1,
                    )
                    for c in range(2)
                ],
                axis=0,
            )
            u = kernel_forward(x, hi_ref[f], lo_ref[f], product) - coefficient * before_ref[f]
            q_ref[f] = u
            square += u * u
            steps.append(u)
        for f in range(FB):
            put_spectra(msg, f, kernel_adjoint(steps[f], khi_ref[f], klo_ref[f]), MSG)
        put_partial(msg, lane_zero(jnp.sum(square, keepdims=True)), MSG)

    pl.when(on_core(0))(lambda: step(thi_ref, tlo_ref, dot))
    pl.when(on_core(1))(lambda: step(khi_ref, klo_ref, dot_nt))


def table_apply(table_ref, at, x):
    hi, lo = split(x)
    both = dot(table_ref[at], jnp.concatenate([hi, lo], axis=1))
    return both[:, :128] + both[:, 128:] + dot(table_ref[at + 1], hi)


def model_kernel(order, last, *refs):
    refs = list(refs)
    recv, cut_ref, table_ref = refs[:3]
    refs = refs[3:]
    stats = refs.pop(0)
    if order > 0:
        earlier = [refs.pop(0) for _ in range(order // 2)]
        total = arrived_sum(recv, MSG)
        spectra = jnp.concatenate([recv[pl.ds(p * MSG, KB), :] for p in range(AF)], axis=0)
    else:
        spectra = recv[...]
    s = table_apply(table_ref, 0, spectra)
    if order > 0:
        s = s - ratio(total, stats[pl.ds(order - 1, 1), :]) * earlier[-1][...]
    cut = cut_ref[pl.ds(lax.rem(lax.axis_index("af"), QB), 1), :]
    keep = lax.broadcasted_iota(jnp.int32, (SAMPLES, 128), 0) < cut
    s = jnp.where(keep, s, 0.0)
    partial = jnp.sum(s * s, axis=0, keepdims=True)
    if order == 0:
        lane = lax.broadcasted_iota(jnp.int32, (1, 128), 1)
        whole = jnp.broadcast_to(jnp.sum(partial, keepdims=True), (1, 128))
        partial = jnp.where(lane == 0, whole, jnp.where(lane == 64, stats[...], 0.0))
    msg = refs.pop(0)
    if not last:
        s_ref = refs.pop(0)
        s_ref[...] = s
    if order > 0:
        [stats_out] = refs
        stats_out[...] = stats[...]
        stats_out[pl.ds(order, 1), :] = total
    if last:
        for j, value in enumerate([e[...] for e in earlier] + [s]):
            for p in range(AF):
                msg[pl.ds(p * LAST + j * TB, TB), :] = value[p * TB : (p + 1) * TB]
        put_partial(msg, partial, LAST)
    else:
        out = table_apply(table_ref, 2, s)
        for p in range(AF):
            msg[pl.ds(p * MSG, KB), :] = out[p * KB : (p + 1) * KB]
        put_partial(msg, partial, MSG)


def stats_kernel(recv, stats, out):
    total = arrived_sum(recv, LAST)
    row = lax.broadcasted_iota(jnp.int32, (8, 128), 0)
    out[...] = jnp.where(row == 5, total, stats[...])


def pair_kernel(mine, other, out):
    out[pl.ds(0, 8), :] = mine[...]
    out[pl.ds(8, 8), :] = other[...]


def last_kernel(recv, g0, g1, g2, g3, q0_ref, q1_ref, q2_ref, sol_out, dir_out, left_out, rows, sol_ref, dir_ref, left_ref, sems):
    gathered = (g0, g1, g2, g3)
    n0, m1, n1, m2, n2, m3 = [
        jnp.concatenate([g[pl.ds(8 * c + j, 1), :] for g in gathered for c in range(2)], axis=0)
        for j in range(6)
    ]

    def norm(x):
        return jnp.sqrt(jnp.sum(x, axis=0, keepdims=True) + EPSILON)

    theta, kappa, lam, mu = ratio(m1, n0), ratio(n1, m1), ratio(m2, n1), ratio(n2, m2)
    beta0 = norm(n0)
    alpha1 = norm(m1 / (beta0 * beta0))
    e = 1.0 / (beta0 * alpha1)
    d = e * theta - alpha1 / beta0
    beta1 = norm(e * e * n1 + d * d * n0)
    f1 = e / beta1
    f0 = d / beta1
    h = f1 * kappa + f0 - beta1 * e
    alpha2 = norm(f1 * f1 * m2 + h * h * m1)
    g2 = f1 / alpha2
    g1 = h / alpha2
    rho1 = jnp.sqrt(alpha1 * alpha1 + beta1 * beta1)
    cos1, sin1 = alpha1 / rho1, beta1 / rho1
    theta1 = sin1 * alpha2
    rhobar = -cos1 * alpha2
    phi1, phibar = cos1 * beta0, sin1 * beta0
    w2 = g2
    w1 = g1 - theta1 / rho1 * e
    c2 = g2
    c1 = g2 * lam + g1 - alpha2 * f1
    c0 = g1 * theta - alpha2 * f0
    beta2 = norm(c2 * c2 * n2 + c1 * c1 * n1 + c0 * c0 * n0)
    c2, c1, c0 = c2 / beta2, c1 / beta2, c0 / beta2
    z3 = c2
    z2 = c2 * mu + c1 - beta2 * g2
    z1 = c1 * kappa + c0 - beta2 * g1
    alpha3 = norm(z3 * z3 * m3 + z2 * z2 * m2 + z1 * z1 * m1)
    rho2 = jnp.sqrt(rhobar * rhobar + beta2 * beta2)
    cos2, sin2 = rhobar / rho2, beta2 / rho2
    step2 = cos2 * phibar / rho2
    turn2 = sin2 * alpha3 / rho2
    x1 = phi1 / rho1 * e + step2 * w1
    x2 = step2 * w2
    y1 = z1 / alpha3 - turn2 * w1
    y2 = z2 / alpha3 - turn2 * w2
    y3 = z3 / alpha3
    for j, value in enumerate((x1, x2, y1, y2, y3, c0, c1, c2)):
        rows[pl.ds(8 * j, 8), :] = jnp.broadcast_to(value, (VERT, 128))
    group = 0
    x1, x2, y1, y2, y3, c0, c1, c2 = [rows[pl.ds(8 * j + group, 1), :] for j in range(8)]
    for v in range(VB):
        for q in range(QB):
            at = (v * QB + q) * LAST
            s1, s2, s3 = [recv[pl.ds(at + j * TB, TB), :] for j in range(3)]
            sol_ref[v, :, q * 128 : (q + 1) * 128] = x1 * s1 + x2 * s2
            dir_ref[v, :, q * 128 : (q + 1) * 128] = y1 * s1 + y2 * s2 + y3 * s3
    copies = [
        pltpu.make_async_copy(sol_ref, sol_out, sems.at[0]),
        pltpu.make_async_copy(dir_ref, dir_out, sems.at[1]),
    ]
    for copy in copies:
        copy.start()
    c0, c1, c2 = c0[:, :1], c1[:, :1], c2[:, :1]
    for f in range(FB):
        left_ref[f] = c0 * q0_ref[f] + c1 * q1_ref[f] + c2 * q2_ref[f]
    copies.append(pltpu.make_async_copy(left_ref, left_out, sems.at[2]))
    copies[-1].start()
    for copy in copies:
        copy.wait()


def call(body, outs, *operands, scratch=(), space=pltpu.VMEM, vmem=16, to=pltpu.VMEM):
    here = pl.BlockSpec(memory_space=to)
    return pl.pallas_call(
        body,
        out_shape=[jax.ShapeDtypeStruct(s, t) for s, t in outs],
        in_specs=[pl.BlockSpec(memory_space=space)] * len(operands),
        out_specs=[here] * len(outs),
        scratch_shapes=list(scratch),
        compiler_params=pltpu.CompilerParams(vmem_limit_bytes=vmem * 1024 * 1024),
    )(*operands)


def exchange(message):
    flat = message.reshape(AF, 1, message.shape[0] // AF * 128)
    flat = lax.all_to_all(flat, "af", split_axis=0, concat_axis=0, tiled=True)
    return flat.reshape(message.shape)


def per_device(recorded, kernel, cutoff):
    tables = jnp.asarray(dft_tables())
    cut = cutoff.reshape(QB, 128)
    kernel = kernel.reshape(FB, 2 * SRCS, RECV)
    message = ((AF * MSG, 128), F32)
    data = ((FB, VB, 2 * SRCS), F32)
    model = ((SAMPLES, 128), F32)
    stat = ((8, 128), F32)
    wide = ((FB, 2 * SRCS, RECV), BF16)

    khi, klo = call(
        halves_kernel,
        [wide, wide],
        kernel,
        scratch=[pltpu.VMEM(kernel.shape, F32), pltpu.SemaphoreType.DMA((len(CHUNKS),))],
        space=pltpu.HBM,
        vmem=49,
    )
    turned_halves = ((FB, RECV, 2 * SRCS), BF16)
    msg, square, thi, tlo = call(
        first_kernel,
        [((AF * KB, 128), F32), ((1, 128), F32), turned_halves, turned_halves],
        recorded, khi, klo,
    )
    msg, s1 = call(
        functools.partial(model_kernel, 0, False),
        [message, model],
        exchange(msg), cut, tables, square,
    )
    msg, q1, stats = call(
        functools.partial(data_kernel, 1),
        [message, data, stat],
        exchange(msg), khi, klo, thi, tlo, recorded, square,
    )
    msg, s2, stats = call(
        functools.partial(model_kernel, 2, False),
        [message, model, stat],
        exchange(msg), cut, tables, stats, s1,
    )
    msg, q2, stats = call(
        functools.partial(data_kernel, 3),
        [message, data, stat],
        exchange(msg), khi, klo, thi, tlo, q1, stats,
    )
    msg, stats = call(
        functools.partial(model_kernel, 4, True),
        [((AF * LAST, 128), F32), stat],
        exchange(msg), cut, tables, stats, s1, s2,
    )
    arrived = exchange(msg)
    [stats] = call(stats_kernel, [stat], arrived, stats)
    [pair] = call(pair_kernel, [((16, 128), F32)], stats, lax.ppermute(stats, "vert", [(i, i ^ 1) for i in range(VERT)]))
    gathered = [pair] + [lax.ppermute(pair, "vert", [(i, i ^ (2 * d)) for i in range(VERT)]) for d in (1, 2, 3)]
    out = ((VB, TB, RECV), F32)
    return tuple(
        call(
            last_kernel,
            [out, out, data],
            arrived, *gathered, recorded, q1, q2,
            scratch=[pltpu.VMEM((64, 128), F32)]
            + [pltpu.VMEM(*o) for o in (out, out, data)]
            + [pltpu.SemaphoreType.DMA((3,))],
            to=pltpu.HBM,
        )
    )


def solution(mesh):
    in_specs = (P("af", "vert", None), P("af", None, None, None), P())
    out_specs = (P("vert", "af", None), P("vert", "af", None), P("af", "vert", None))
    return jax.shard_map(
        per_device, mesh=mesh, in_specs=in_specs, out_specs=out_specs, check_vma=False
    )
```
